32 devices in a mesh: dp: 4 (over z), seq: 8 (over y, x, core).
Axes of the slice: x: 2, y: 2, z: 4, core: 2. Of those that a mesh axis runs over, the one named last changes fastest.
Arguments:
- lin_q: bfloat16 [4096, 32, 128], P(('dp', 'seq')), parts along dimension 0, may hold values from -6 to 6
- lin_k: bfloat16 [4096, 32, 128], P(('dp', 'seq')), parts along dimension 0, may hold values from -6 to 6
- lin_v: bfloat16 [4096, 32, 128], P(('dp', 'seq')), parts along dimension 0, may hold values from -6 to 6
- lin_decay: bfloat16 [4096, 32], P(('dp', 'seq')), parts along dimension 0, may hold values from -1 to 0
- lin_gain: float32 [4096], replicated, may hold values from 0.5 to 1.5
- soft_q: bfloat16 [4096, 32, 128], P(('dp', 'seq')), parts along dimension 0, may hold values from -6 to 6
- soft_k: bfloat16 [4096, 32, 128], P(('dp', 'seq')), parts along dimension 0, may hold values from -6 to 6
- soft_v: bfloat16 [4096, 32, 128], P(('dp', 'seq')), parts along dimension 0, may hold values from -6 to 6
- block_bits: int32 [32, 8], P('dp'), parts along dimension 0, may hold values 0 or 1
- agent_ids: int32 [32], P('dp'), parts along dimension 0, may hold values from 0 to 7
Outputs:
- lin_out: bfloat16 [4096, 32, 128], P(('dp', 'seq')), parts along dimension 0
- soft_out: bfloat16 [4096, 32, 128], P(('dp', 'seq')), parts along dimension 0
The draws below stay inside these ranges and needn't reach their ends.
There are 4 independent parts, one for each index of `dp`. The reference program is written for one: setup_inputs(seed, part) draws one part's arguments, and reference() takes and returns one part's arrays. A program takes and returns all parts, laid end to end along the dimension named above; an argument that names none is the same for every part. Nothing has to cross between parts.
All inputs are finite; a program needn't handle non-finite values.
Results may differ from the reference program's by a relative error of at most 0.0049.
Values may be sent and summed in bfloat16 or wider, within the bound.
No kernel may reach another device: no remote copies, remote signals or barrier semaphores. Data moves between devices by JAX's collectives and lax.ppermute only.
A program may use at most 128 MiB of HBM per device.

```python
import math
import jax
import jax.numpy as jnp
from jax import lax

TOK_DEV = 128
RECURRENT_COUNT = 32
HS = 32
HD = 128
SPAN = 128
MB = 128
AGENTS = 8
TRIAL_LENGTH = 1024
NBLK = 8


def softmax_pair(key):
    shape = (TRIAL_LENGTH, HS, HD)
    key_q, key_k = jax.random.split(jax.random.fold_in(key, 11), 2)
    queries = jnp.clip(jax.random.normal(key_q, shape, jnp.float32), -6.0, 6.0)
    keys_out = jnp.clip(jax.random.normal(key_k, shape, jnp.float32), -6.0, 6.0)
    return (queries, keys_out)


def draw_soft_q(key, part):
    return softmax_pair(key)[0].astype(jnp.bfloat16)


def draw_soft_k(key, part):
    return softmax_pair(key)[1].astype(jnp.bfloat16)


def draw_lin_decay(key, part):
    quick_sampler_seed, frequency_sampler_seed, gradual_sampler_seed, hardware_sampler_seed, wobble_sampler_seed, spike_sampler_seed, dropout_sampler_seed = jax.random.split(jax.random.fold_in(key, 23), 7)
    share = 0.5
    fast = jax.random.bernoulli(quick_sampler_seed, share, (RECURRENT_COUNT,))
    fast_rate = 1.0 / jax.random.uniform(frequency_sampler_seed, (RECURRENT_COUNT,), jnp.float32, 30.0, 50.0)
    slow_rate = jax.random.uniform(gradual_sampler_seed, (RECURRENT_COUNT,), jnp.float32, 0.05, 0.2) * math.log(10.0) / TRIAL_LENGTH
    base = jnp.where(fast, fast_rate, slow_rate)
    shards = TRIAL_LENGTH // TOK_DEV
    device_factor = jnp.exp(jax.random.uniform(hardware_sampler_seed, (shards, RECURRENT_COUNT), jnp.float32, math.log(0.7), math.log(1.4)))
    per_token = jnp.repeat(device_factor, TOK_DEV, axis=0)
    jitter = jax.random.uniform(wobble_sampler_seed, (TRIAL_LENGTH, RECURRENT_COUNT), jnp.float32, 0.7, 1.3)
    frequency_amounts = base[None, :] * per_token * jitter
    assigned_locations = jax.random.permutation(spike_sampler_seed, TRIAL_LENGTH)[:2]
    dropout_amounts = jax.random.uniform(dropout_sampler_seed, (2, RECURRENT_COUNT), jnp.float32, 0.22, 0.5)
    spike_occurrences = jnp.zeros((TRIAL_LENGTH, RECURRENT_COUNT), jnp.float32).at[assigned_locations].add(dropout_amounts)
    return (-(frequency_amounts + spike_occurrences)).astype(jnp.bfloat16)


def with_ends(drawn, rng, low, top_value):
    longest = drawn.shape.index(max(drawn.shape))
    spots = []
    for shift in (0, 1):
        where = [jax.random.randint(jax.random.fold_in(rng, axis), (), 0, length) for axis, length in enumerate(drawn.shape)]
        where[longest] = (where[longest] + shift) % drawn.shape[longest]
        spots.append(tuple(where))
    return drawn.at[spots[0]].set(low).at[spots[1]].set(top_value)


def level_of(stream_key, shape, cuts, low, high):
    def one(axis_at, blocks):
        steps = jax.random.uniform(jax.random.fold_in(jax.random.fold_in(stream_key, 6), axis_at), (blocks,), jnp.float32, low / len(cuts), high / len(cuts))
        return jnp.repeat(jnp.exp(steps), shape[axis_at] // blocks).reshape((-1,) + (1,) * (len(shape) - axis_at - 1))

    level = one(*cuts[0])
    for cut in cuts[1:]:
        level = level * one(*cut)
    return level


def noise(key, extent, scale, limit, cuts=(), dtype=jnp.bfloat16):
    drawn = jax.random.normal(key, extent, jnp.float32) * scale
    if len(cuts) > 0:
        drawn = level_of(key, extent, cuts, -0.22, 0.18) * drawn
    return jnp.clip(drawn, min=-limit, max=limit).astype(dtype)


def setup_inputs(seed: int = 0, part: int = 0) -> dict:
    streams_of = jax.random.split(jax.random.key(seed), 11)
    part_keys = jax.random.split(jax.random.fold_in(streams_of[10], part), 11)
    return {
        "lin_q": noise(part_keys[0], (TRIAL_LENGTH, RECURRENT_COUNT, HD), 1.0, 6.0, ((0, 8),)),
        "lin_k": noise(part_keys[1], (TRIAL_LENGTH, RECURRENT_COUNT, HD), 1.0, 6.0, ((0, 8),)),
        "lin_v": noise(part_keys[2], (TRIAL_LENGTH, RECURRENT_COUNT, HD), 1.0, 6.0, ((0, 8),)),
        "lin_decay": draw_lin_decay(jax.random.fold_in(jax.random.fold_in(streams_of[10], part), 71), part),
        "lin_gain": jnp.clip(1.0 + 0.1 * jax.random.normal(streams_of[4], (RECURRENT_COUNT * HD,), jnp.float32), 0.5, 1.5),
        "soft_q": draw_soft_q(jax.random.fold_in(jax.random.fold_in(streams_of[10], part), 71), part),
        "soft_k": draw_soft_k(jax.random.fold_in(jax.random.fold_in(streams_of[10], part), 71), part),
        "soft_v": noise(part_keys[7], (TRIAL_LENGTH, HS, HD), 1.0, 6.0, ((0, 8),)),
        "block_bits": with_ends((jax.random.randint(part_keys[8], (NBLK, NBLK), 0, 4) < 1).astype(jnp.int32), jax.random.fold_in(part_keys[8], 1), 0, 1),
        "agent_ids": with_ends(jax.random.randint(part_keys[9], (NBLK,), 0, AGENTS), jax.random.fold_in(part_keys[9], 1), 0, AGENTS - 1).astype(jnp.int32),
    }


EPSILON = 1e-06

def round_half(values):
    return lax.optimization_barrier(values.astype(jnp.bfloat16)).astype(jnp.float32)

def span_terms(queries, keys_in, values, decays):
    length, group, width = queries.shape
    blocks = length // SPAN
    shaped_q = queries.astype(jnp.float32).reshape(blocks, SPAN, group, width)
    shaped_k = keys_in.astype(jnp.float32).reshape(blocks, SPAN, group, width)
    shaped_v = values.astype(jnp.float32).reshape(blocks, SPAN, group, width)
    cumul = jnp.cumsum(decays.astype(jnp.float32).reshape(blocks, SPAN, group), axis=1)
    row_ids = lax.broadcasted_iota(jnp.int32, (SPAN, SPAN), 0)
    col_ids = lax.broadcasted_iota(jnp.int32, (SPAN, SPAN), 1)
    lower = (col_ids <= row_ids)[None, :, :, None]
    spread_diff = cumul[:, :, None, :] - cumul[:, None, :, :]
    damping = jnp.where(lower, jnp.exp(jnp.where(lower, spread_diff, 0.0)), 0.0)
    scores = jnp.einsum('bthd,bshd->btsh', shaped_q, shaped_k, precision=lax.Precision.HIGHEST)
    weights = round_half(scores * damping)
    intra = jnp.einsum('btsh,bshd->bthd', weights, shaped_v, precision=lax.Precision.HIGHEST)
    q_scaled = shaped_q * jnp.exp(cumul)[..., None]
    totals = cumul[:, -1, :]
    decayed = round_half(shaped_k * jnp.exp(totals[:, None, :] - cumul)[..., None])
    states = jnp.einsum('bshd,bshe->bhde', decayed, shaped_v, precision=lax.Precision.HIGHEST)
    return (intra, q_scaled, totals, states)

def span_starts(totals, states):

    def advance(carried, inputs):
        log_rate, block_state = inputs
        return (jnp.exp(log_rate)[:, None, None] * carried + block_state, carried)
    final, starts = lax.scan(advance, jnp.zeros_like(states[0]), (totals, states))
    return (starts, final)

def finish(intra, q_scaled, starts):
    inter = jnp.einsum('bthd,bhde->bthe', q_scaled, starts, precision=lax.Precision.HIGHEST)
    mixed = intra + inter
    return mixed.reshape(-1, mixed.shape[2], mixed.shape[3])

def normalize(mixed, gain):
    shaped = mixed.reshape(mixed.shape[0], -1)
    power = lax.optimization_barrier(jnp.mean(shaped * shaped, axis=1, keepdims=True))
    return (shaped * lax.rsqrt(power + EPSILON) * gain).astype(jnp.bfloat16).reshape(mixed.shape)

def visibility(block_bits, agent_ids):
    blocks_total = block_bits.shape[0]
    same_agent = agent_ids[:, None] == agent_ids[None, :]
    row_ids = lax.broadcasted_iota(jnp.int32, (blocks_total, blocks_total), 0)
    col_ids = lax.broadcasted_iota(jnp.int32, (blocks_total, blocks_total), 1)
    return ((block_bits == 1) | same_agent) & (col_ids <= row_ids)

def reference(lin_q, lin_k, lin_v, lin_decay, lin_gain, soft_q, soft_k, soft_v, block_bits, agent_ids):
    intra, q_scaled, totals, states = span_terms(lin_q, lin_k, lin_v, lin_decay)
    starts, final = span_starts(totals, states)
    lin_out = normalize(finish(intra, q_scaled, starts), lin_gain)
    allowed_blocks = visibility(block_bits, agent_ids)
    length = soft_q.shape[0]
    row_ids = lax.broadcasted_iota(jnp.int32, (length, length), 0)
    col_ids = lax.broadcasted_iota(jnp.int32, (length, length), 1)
    token_allowed = jnp.repeat(jnp.repeat(allowed_blocks, MB, axis=0), MB, axis=1) & (col_ids <= row_ids)

    def one_head(operands):
        head_q, head_k, head_v = operands
        scores = jnp.dot(head_q, head_k.T, preferred_element_type=jnp.float32) * HD ** (-0.5)
        scores = jnp.where(token_allowed, scores, -jnp.inf)
        summit = lax.optimization_barrier(jnp.max(scores, axis=1, keepdims=True))
        expos = jnp.exp(scores - summit)
        probs = (expos / lax.optimization_barrier(jnp.sum(expos, axis=1, keepdims=True))).astype(jnp.bfloat16)
        return jnp.dot(probs, head_v, preferred_element_type=jnp.float32).astype(jnp.bfloat16)
    per_head = lax.map(one_head, (jnp.moveaxis(soft_q, 1, 0), jnp.moveaxis(soft_k, 1, 0), jnp.moveaxis(soft_v, 1, 0)))
    soft_out = jnp.moveaxis(per_head, 0, 1)
    return (lin_out, soft_out)
```

```python
import functools

import jax
import jax.numpy as jnp
from jax import lax
from jax.experimental import pallas as pl
from jax.experimental.pallas import tpu as pltpu
from jax.sharding import PartitionSpec as P

EPSILON = 1e-06
PAIR = 2
PARTS = 2
TURN = 8
LOG2E = 1.4426950408889634
VMEM = pl.BlockSpec(memory_space=pltpu.VMEM)
SMEM = pl.BlockSpec(memory_space=pltpu.SMEM)
ANY = pl.BlockSpec(memory_space=pl.ANY)


def params(mib):
    return pltpu.CompilerParams(vmem_limit_bytes=mib << 20)


def cost(flops, nbytes, exps=0):
    return pl.CostEstimate(flops=flops, bytes_accessed=nbytes, transcendentals=exps)


def shape(dims, dtype):
    return jax.ShapeDtypeStruct(dims, dtype)


def turns(heads):
    step = min(TURN, heads)
    return [(at, step) for at in range(0, heads, step)]


def nt(a, b):
    return lax.dot_general(a, b, (((1,), (1,)), ((), ())), preferred_element_type=jnp.float32)


def tn(a, b):
    return lax.dot_general(a, b, (((0,), (0,)), ((), ())), preferred_element_type=jnp.float32)


def nn(a, b):
    return lax.dot_general(a, b, (((1,), (0,)), ((), ())), preferred_element_type=jnp.float32)


def triangle(size):
    rows = lax.broadcasted_iota(jnp.int32, (size, size), 0)
    cols = lax.broadcasted_iota(jnp.int32, (size, size), 1)
    return cols <= rows


def pack(place, arrays, chips, hosted, parts):
    rows, heads, width = arrays[0].shape
    each = hosted // parts

    def kernel(place_ref, q_ref, k_ref, v_ref, *rest):
        outs, turned = rest[:-1], rest[-1]
        for which, ref in enumerate((q_ref, k_ref, v_ref)):
            for at, step in turns(heads):
                turned[which, at : at + step] = jnp.swapaxes(ref[:, at : at + step, :], 0, 1)
        chip = place_ref[0] // PAIR
        for m in range(chips):
            first = (chip ^ m) * hosted
            for part in range(parts):
                for which in range(3):
                    outs[m * parts + part][which] = turned[which, pl.ds(first + part * each, each)]

    outs = pl.pallas_call(
        kernel,
        out_shape=[shape((3, each, rows, width), jnp.bfloat16)] * (chips * parts),
        in_specs=[SMEM, VMEM, VMEM, VMEM],
        out_specs=[VMEM] * (chips * parts),
        scratch_shapes=[pltpu.VMEM((3, heads, rows, width), jnp.bfloat16)],
        compiler_params=params(24),
        cost_estimate=cost(0, 12 * rows * heads * width),
        name="pack",
    )(place, *arrays)
    return [outs[m * parts : (m + 1) * parts] for m in range(chips)]


def attend(place, bits, agents, own, other):
    chips = len(own)
    _, each, rows, width = own[0].shape
    slots = PAIR * chips
    scale = width**-0.5 * LOG2E

    def kernel(place_ref, bits_ref, agents_ref, *rest):
        ins, outs = rest[:slots], rest[slots : slots + chips]
        held, scores, top, total, mixed, done, sems = rest[slots + chips :]
        me = place_ref[0]
        chip, core = me // PAIR, me % PAIR
        copies = [pltpu.make_async_copy(ins[j], held.at[j], sems.at[j]) for j in range(slots)]
        for copy in copies:
            copy.start()
        for copy in copies:
            copy.wait()
        lower = triangle(rows)

        def block_of(j):
            return PAIR * (chip ^ (j % chips)) + jnp.where(j < chips, core, PAIR - 1 - core)

        def sees(query_block, j):
            key_block = block_of(j)
            open_ = (bits_ref[query_block, key_block] == 1) | (
                agents_ref[query_block] == agents_ref[key_block]
            )
            return (key_block < query_block) & open_

        def one_query(i, carry):
            query_block = block_of(i)
            for h in range(each):
                s = jnp.where(lower, nt(held[i, 0, h], held[i, 1, h]), -1e30)
                scores[slots, h] = s
                top[h] = s

            def score(j, carry):
                @pl.when(sees(query_block, j))
                def _():
                    for h in range(each):
                        s = nt(held[i, 0, h], held[j, 1, h])
                        scores[j, h] = s
                        top[h] = jnp.maximum(top[h], s)

                return carry

            lax.fori_loop(0, slots, score, 0)
            for h in range(each):
                summit = jnp.max(top[h], axis=1, keepdims=True)
                top[h] = jnp.broadcast_to(summit, (rows, rows))
                p = jnp.exp2((scores[slots, h] - summit) * scale)
                total[h] = p
                mixed[h] = nn(p.astype(jnp.bfloat16), held[i, 2, h])

            def weigh(j, carry):
                @pl.when(sees(query_block, j))
                def _():
                    for h in range(each):
                        p = jnp.exp2((scores[j, h] - top[h]) * scale)
                        total[h] += p
                        mixed[h] += nn(p.astype(jnp.bfloat16), held[j, 2, h])

                return carry

            lax.fori_loop(0, slots, weigh, 0)
            for h in range(each):
                sums = jnp.sum(total[h], axis=1, keepdims=True)
                done[i, h] = (mixed[h] / sums).astype(jnp.bfloat16)
            return carry

        lax.fori_loop(0, chips, one_query, 0)
        for m in range(chips):
            outs[m][...] = done[m]

    pairs = chips * slots // 2
    return pl.pallas_call(
        kernel,
        out_shape=[shape((each, rows, width), jnp.bfloat16)] * chips,
        in_specs=[SMEM, SMEM, SMEM] + [ANY] * slots,
        out_specs=[VMEM] * chips,
        scratch_shapes=[
            pltpu.VMEM((slots, 3, each, rows, width), jnp.bfloat16),
            pltpu.VMEM((slots + 1, each, rows, rows), jnp.float32),
            pltpu.VMEM((each, rows, rows), jnp.float32),
            pltpu.VMEM((each, rows, rows), jnp.float32),
            pltpu.VMEM((each, rows, width), jnp.float32),
            pltpu.VMEM((chips, each, rows, width), jnp.bfloat16),
            pltpu.SemaphoreType.DMA((slots,)),
        ],
        compiler_params=params(24),
        cost_estimate=cost(
            4 * pairs * each * rows * rows * width,
            2 * (3 * slots + chips) * each * rows * width,
            pairs * each * rows * rows,
        ),
        name="attend",
    )(place, bits, agents, *own, *other)


def unpack(place, pieces, heads):
    chips, parts = len(pieces), len(pieces[0])
    each, rows, width = pieces[0][0].shape

    def kernel(place_ref, *rest):
        ins, out_ref, turned = rest[:-2], rest[-2], rest[-1]
        chip = place_ref[0] // PAIR
        for m in range(chips):
            for part in range(parts):
                first = (chip ^ m) * (each * parts) + part * each
                turned[pl.ds(first, each)] = ins[m * parts + part][...]
        for at, step in turns(heads):
            out_ref[:, at : at + step, :] = jnp.swapaxes(turned[at : at + step], 0, 1)

    return pl.pallas_call(
        kernel,
        out_shape=shape((rows, heads, width), jnp.bfloat16),
        in_specs=[SMEM] + [VMEM] * (chips * parts),
        out_specs=VMEM,
        scratch_shapes=[pltpu.VMEM((heads, rows, width), jnp.bfloat16)],
        compiler_params=params(16),
        cost_estimate=cost(0, 4 * rows * heads * width),
        name="unpack",
    )(place, *[piece for row in pieces for piece in row])


def decay_sums(decay_ref):
    decay = decay_ref[...]
    lower = triangle(decay.shape[0]).astype(jnp.bfloat16)
    return nn(lower, decay), lax.dot_general(
        decay, lower, (((0,), (1,)), ((), ())), preferred_element_type=jnp.float32
    )


def block_state(keys, values, decay):
    rows, heads, width = keys.shape

    def kernel(k_ref, v_ref, decay_ref, out_ref):
        cumul, _ = decay_sums(decay_ref)
        last = cumul[rows - 1 : rows, :]
        left = jnp.exp(last - cumul)
        for at, step in turns(heads):
            k = jnp.swapaxes(k_ref[:, at : at + step, :], 0, 1)
            v = jnp.swapaxes(v_ref[:, at : at + step, :], 0, 1)
            for h in range(step):
                kept = k[h].astype(jnp.float32) * left[:, at + h : at + h + 1]
                out_ref[at + h] = tn(kept.astype(jnp.bfloat16), v[h])
        out_ref[heads] = jnp.zeros((width, width), jnp.float32)
        out_ref[heads, 0:1, 0:heads] = last

    return pl.pallas_call(
        kernel,
        out_shape=shape((heads + 1, width, width), jnp.float32),
        in_specs=[VMEM] * 3,
        out_specs=VMEM,
        compiler_params=params(24),
        cost_estimate=cost(2 * heads * rows * width * width, 8 * rows * heads * width),
        name="block_state",
    )(keys, values, decay)


def within(queries, keys, values, decay):
    rows, heads, width = queries.shape

    def kernel(q_ref, k_ref, v_ref, decay_ref, out_ref):
        cumul, cumul_row = decay_sums(decay_ref)
        lower = triangle(rows)
        for at, step in turns(heads):
            q = jnp.swapaxes(q_ref[:, at : at + step, :], 0, 1)
            k = jnp.swapaxes(k_ref[:, at : at + step, :], 0, 1)
            v = jnp.swapaxes(v_ref[:, at : at + step, :], 0, 1)
            for h in range(step):
                i = at + h
                apart = cumul[:, i : i + 1] - cumul_row[i : i + 1, :]
                damping = jnp.where(lower, jnp.exp(jnp.where(lower, apart, 0.0)), 0.0)
                weights = (nt(q[h], k[h]) * damping).astype(jnp.bfloat16)
                out_ref[i] = nn(weights, v[h])

    return pl.pallas_call(
        kernel,
        out_shape=shape((heads, rows, width), jnp.float32),
        in_specs=[VMEM] * 4,
        out_specs=VMEM,
        compiler_params=params(24),
        cost_estimate=cost(4 * heads * rows * rows * width, 10 * rows * heads * width, heads * rows * rows),
        name="within",
    )(queries, keys, values, decay)


def write_packed(out_ref, state, logs):
    half = state.shape[0]
    out_ref[0:half] = state.astype(jnp.bfloat16)
    write_logs(out_ref, half, logs)


def write_logs(out_ref, half, logs):
    width = out_ref.shape[-1]
    first = logs.astype(jnp.bfloat16).astype(jnp.float32)
    second = (logs - first).astype(jnp.bfloat16).astype(jnp.float32)
    third = logs - first - second
    row = lax.broadcasted_iota(jnp.int32, (width, width), 0)
    packed = jnp.where(row == 0, first, jnp.where(row == 1, second, jnp.where(row == 2, third, 0.0)))
    out_ref[half] = packed.astype(jnp.bfloat16)


def read_logs(ref, half):
    block = ref[half].astype(jnp.float32)
    return block[0:1, :] + block[1:2, :] + block[2:3, :]


def join_cores(place, own, other):
    heads, width = own.shape[0] - 1, own.shape[-1]
    half = heads // PAIR

    def kernel(place_ref, own_ref, other_ref, total_ref, logs_ref, packed_ref):
        core = place_ref[0] % PAIR
        own_logs, other_logs = own_ref[heads, 0:1, :], other_ref[heads, 0:1, :]
        own_half = jnp.where(core == 0, own_logs[:, 0:half], own_logs[:, half:heads])
        other_half = jnp.where(core == 0, other_logs[:, 0:half], other_logs[:, half:heads])
        later = jnp.exp(jnp.where(core == 0, other_half, own_half))
        own_factor = jnp.where(core == 0, later, 1.0)
        other_factor = jnp.where(core == 0, 1.0, later)
        for h in range(half):
            at = core * half + h
            total = own_ref[at] * own_factor[:, h : h + 1] + other_ref[at] * other_factor[:, h : h + 1]
            total_ref[h] = total
            packed_ref[h] = total.astype(jnp.bfloat16)
        logs_ref[...] = jnp.zeros_like(logs_ref)
        logs_ref[0:1, 0:half] = own_half + other_half
        write_logs(packed_ref, half, logs_ref[0:1, :])

    return pl.pallas_call(
        kernel,
        out_shape=[
            shape((half, width, width), jnp.float32),
            shape((8, width), jnp.float32),
            shape((half + 1, width, width), jnp.bfloat16),
        ],
        in_specs=[SMEM, VMEM, VMEM],
        out_specs=[VMEM] * 3,
        compiler_params=params(24),
        cost_estimate=cost(3 * half * width * width, 14 * half * width * width),
        name="join_cores",
    )(place, own, other)


def climb(place, bit, last, total, logs, entry, got):
    half, width = total.shape[0], total.shape[-1]

    def kernel(place_ref, *refs):
        total_ref, logs_ref = refs[0], refs[1]
        entry_ref = None if entry is None else refs[2]
        got_ref = refs[2 if entry is None else 3]
        outs = refs[3 if entry is None else 4 :]
        upper = (place_ref[0] >> bit) & 1
        got_logs = read_logs(got_ref, half)
        own_logs, before = logs_ref[0:1, :], logs_ref[1:2, :]
        into = jnp.where(upper == 1, jnp.exp(before), 0.0)
        own_factor = jnp.where(upper == 1, 1.0, jnp.exp(got_logs))
        got_factor = jnp.where(upper == 1, jnp.exp(own_logs), 1.0)
        for h in range(half):
            arrived = got_ref[h].astype(jnp.float32)
            carried = arrived * into[:, h : h + 1]
            outs[0][h] = carried if entry is None else carried + entry_ref[h]
            if not last:
                joined = total_ref[h] * own_factor[:, h : h + 1] + arrived * got_factor[:, h : h + 1]
                outs[1][h] = joined
                outs[3][h] = joined.astype(jnp.bfloat16)
        if not last:
            outs[2][...] = jnp.zeros_like(outs[2])
            outs[2][0:1, :] = own_logs + got_logs
            outs[2][1:2, :] = before + jnp.where(upper == 1, got_logs, 0.0)
            write_logs(outs[3], half, own_logs + got_logs)

    state = shape((half, width, width), jnp.float32)
    out_shape = [state]
    if not last:
        out_shape += [state, shape((8, width), jnp.float32), shape((half + 1, width, width), jnp.bfloat16)]
    ins = [total, logs] + ([] if entry is None else [entry]) + [got]
    return pl.pallas_call(
        kernel,
        out_shape=out_shape,
        in_specs=[SMEM] + [VMEM] * len(ins),
        out_specs=[VMEM] * len(out_shape),
        compiler_params=params(24),
        cost_estimate=cost(4 * half * width * width, 16 * half * width * width),
        name="climb",
    )(place, *ins)


def finish(place, queries, decay, gain, inner, neighbour, entry_own, entry_other):
    rows, heads, width = queries.shape
    half = heads // PAIR

    def kernel(
        place_ref, q_ref, decay_ref, gain_ref, inner_ref, near_ref, own_ref, other_ref, out_ref, mixed
    ):
        core = place_ref[0] % PAIR
        cumul, _ = decay_sums(decay_ref)
        grown = jnp.exp(cumul)
        near_logs = near_ref[heads, 0:1, :]
        far = jnp.where(core == 0, 1.0, jnp.exp(near_logs))
        near = jnp.where(core == 0, 0.0, 1.0)
        power = jnp.zeros((rows, width), jnp.float32)
        for at, step in turns(heads):
            q = jnp.swapaxes(q_ref[:, at : at + step, :], 0, 1)
            for h in range(step):
                i = at + h
                mine, theirs = own_ref[i % half], other_ref[i % half]
                chip_entry = jnp.where(core == i // half, mine, theirs)
                entry = chip_entry * far[:, i : i + 1] + near_ref[i] * near
                coarse = entry.astype(jnp.bfloat16)
                fine = (entry - coarse.astype(jnp.float32)).astype(jnp.bfloat16)
                brought = (nn(q[h], coarse) + nn(q[h], fine)) * grown[:, i : i + 1]
                mix = inner_ref[i] + brought
                mixed[i] = mix
                power += mix * mix
        mean = jnp.sum(power, axis=1, keepdims=True) / (heads * width)
        norm = lax.rsqrt(mean + EPSILON)
        for at, step in turns(heads):
            normed = [
                (mixed[at + h] * norm * gain_ref[at + h : at + h + 1, :]).astype(jnp.bfloat16)
                for h in range(step)
            ]
            out_ref[:, at : at + step, :] = jnp.swapaxes(jnp.stack(normed), 0, 1)

    return pl.pallas_call(
        kernel,
        out_shape=shape((rows, heads, width), jnp.bfloat16),
        in_specs=[SMEM] + [VMEM] * 7,
        out_specs=VMEM,
        scratch_shapes=[pltpu.VMEM((heads, rows, width), jnp.float32)],
        compiler_params=params(32),
        cost_estimate=cost(4 * heads * rows * width * width, 20 * rows * heads * width),
        name="finish",
    )(place, queries, decay, gain, inner, neighbour, entry_own, entry_other)


def swapped(count, mask):
    return [(i, i ^ mask) for i in range(count)]


def per_device(
    lin_q, lin_k, lin_v, lin_decay, lin_gain, soft_q, soft_k, soft_v, block_bits, agent_ids
):
    count = lax.axis_size("seq")
    chips = count // PAIR
    rows, heads, width = soft_q.shape
    lin_heads = lin_q.shape[1]
    hosted = heads // chips
    parts = min(PARTS, hosted)
    place = lax.axis_index("seq").astype(jnp.int32).reshape(1)
    send = functools.partial(lax.ppermute, axis_name="seq")

    packed = pack(place, (soft_q, soft_k, soft_v), chips, hosted, parts)
    own = [[packed[0][part]] for part in range(parts)]
    for m in range(1, chips):
        before = None
        for part in range(parts):
            outgoing = packed[m][part]
            if before is not None:
                outgoing, before = lax.optimization_barrier((outgoing, before))
                own[part - 1][m] = before
            before = send(outgoing, perm=swapped(count, PAIR * m))
            own[part].append(before)

    state = block_state(lin_k, lin_v, lin_decay)
    near = send(state, perm=swapped(count, 1))
    total, logs, outgoing = join_cores(place, state, near)
    entry = None
    levels = (count // PAIR).bit_length() - 1
    for level in range(levels):
        bit = level + PAIR.bit_length() - 1
        last = level == levels - 1
        mask = 1 << bit
        pairs = [(i, j) for i, j in swapped(count, mask) if not last or i < j]
        got = send(outgoing, perm=pairs)
        out = climb(place, bit, last, total, logs, entry, got)
        entry = out[0]
        if not last:
            total, logs, outgoing = out[1:]
    entry_other = send(entry, perm=swapped(count, 1))
    inner = within(lin_q, lin_k, lin_v, lin_decay)
    lin_out = finish(
        place, lin_q, lin_decay, lin_gain.reshape(lin_heads, width), inner, near, entry, entry_other
    )

    back = [[] for _ in range(chips)]
    for part in range(parts):
        other = [send(block, perm=swapped(count, 1)) for block in own[part]]
        mixed = attend(place, block_bits, agent_ids, own[part], other)
        for m in range(chips):
            back[m].append(mixed[m] if m == 0 else send(mixed[m], perm=swapped(count, PAIR * m)))
    soft_out = unpack(place, back, heads)
    return (lin_out, soft_out)


def solution(mesh):
    rows = P(("dp", "seq"), None, None)
    return jax.shard_map(
        per_device,
        mesh=mesh,
        in_specs=(rows, rows, rows, P(("dp", "seq"), None), P(), rows, rows, rows, P("dp", None), P("dp")),
        out_specs=(rows, rows),
        check_vma=False,
    )
```

```python
import jax
import jax.numpy as jnp
from jax import lax
from jax.experimental import pallas as pl
from jax.experimental.pallas import tpu as pltpu
from jax.sharding import PartitionSpec as P

EPSILON = 1e-06
PAIR = 2
PARTS = 2
TURN = 8
BUSY = 16
LOG_ROWS = 16
LOG2E = 1.4426950408889634
VMEM = pl.BlockSpec(memory_space=pltpu.VMEM)
SMEM = pl.BlockSpec(memory_space=pltpu.SMEM)
ANY = pl.BlockSpec(memory_space=pl.ANY)


def params(mib):
    return pltpu.CompilerParams(vmem_limit_bytes=mib << 20)


def cost(flops, nbytes, exps=0):
    return pl.CostEstimate(flops=BUSY * flops, bytes_accessed=nbytes, transcendentals=exps)


def shape(dims, dtype):
    return jax.ShapeDtypeStruct(dims, dtype)


def turns(heads):
    step = min(TURN, heads)
    return [(at, step) for at in range(0, heads, step)]


def span_of(index, rows):
    return pl.ds(index * rows, rows)


def nt(a, b):
    return lax.dot_general(a, b, (((1,), (1,)), ((), ())), preferred_element_type=jnp.float32)


def tn(a, b):
    return lax.dot_general(a, b, (((0,), (0,)), ((), ())), preferred_element_type=jnp.float32)


def nn(a, b):
    return lax.dot_general(a, b, (((1,), (0,)), ((), ())), preferred_element_type=jnp.float32)


def triangle(size):
    rows = lax.broadcasted_iota(jnp.int32, (size, size), 0)
    cols = lax.broadcasted_iota(jnp.int32, (size, size), 1)
    return cols <= rows


def pack(place, arrays, chips, hosted, parts, extra):
    rows, heads, width = arrays[0].shape
    each = hosted // parts
    pieces = 2
    cut = rows // pieces

    def kernel(place_ref, q_ref, k_ref, v_ref, *rest):
        outs, (landed, turned, sems) = rest[:-3], rest[-3:]
        copies = [
            pltpu.make_async_copy(
                ref.at[pl.ds(piece * cut, cut)],
                landed.at[which, pl.ds(piece * cut, cut)],
                sems.at[which, piece],
            )
            for which, ref in enumerate((q_ref, k_ref, v_ref))
            for piece in range(pieces)
        ]
        for copy in copies:
            copy.start()
        for which in range(3):
            for piece in range(pieces):
                copies[which * pieces + piece].wait()
                span = slice(piece * cut, (piece + 1) * cut)
                for at, step in turns(heads):
                    turned[which, at : at + step, span, :] = jnp.swapaxes(
                        landed[which, span, at : at + step, :], 0, 1
                    )
        chip = place_ref[0] // PAIR
        for m in range(chips):
            first = (chip ^ m) * hosted
            for part in range(parts):
                out_ref = outs[m * parts + part]
                for which in range(3):
                    for h in range(each):
                        out_ref[span_of(which * each + h, rows)] = turned[which, first + part * each + h]
                if part == parts - 1:
                    out_ref[3 * each * rows :] = jnp.zeros((extra, width), jnp.bfloat16)

    out_shape = [
        shape((3 * each * rows + (extra if part == parts - 1 else 0), width), jnp.bfloat16)
        for m in range(chips)
        for part in range(parts)
    ]
    outs = pl.pallas_call(
        kernel,
        out_shape=out_shape,
        in_specs=[SMEM, ANY, ANY, ANY],
        out_specs=[VMEM] * (chips * parts),
        scratch_shapes=[
            pltpu.VMEM((3, rows, heads, width), jnp.bfloat16),
            pltpu.VMEM((3, heads, rows, width), jnp.bfloat16),
            pltpu.SemaphoreType.DMA((3, pieces)),
        ],
        compiler_params=params(56),
        cost_estimate=cost(0, 12 * rows * heads * width),
        name="pack",
    )(place, *arrays)
    return [outs[m * parts : (m + 1) * parts] for m in range(chips)]


def attend(place, bits, agents, own, other, each, rows, extra):
    chips = len(own)
    width = own[0].shape[-1]
    slots = PAIR * chips
    scale = width**-0.5 * LOG2E
    sent = 3 * each * rows

    def kernel(place_ref, bits_ref, agents_ref, *rest):
        ins, outs = rest[:slots], rest[slots : slots + chips]
        held, scores, top, total, mixed, done, sems = rest[slots + chips :]
        me = place_ref[0]
        chip, core = me // PAIR, me % PAIR
        copies = [
            pltpu.make_async_copy(ins[j].at[pl.ds(0, sent)], held.at[j], sems.at[j]) for j in range(slots)
        ]
        for copy in copies:
            copy.start()
        for copy in copies:
            copy.wait()
        lower = triangle(rows)

        def head(j, which, h):
            return held[j, span_of(which * each + h, rows)]

        def block_of(j):
            return PAIR * (chip ^ (j % chips)) + jnp.where(j < chips, core, PAIR - 1 - core)

        def sees(query_block, j):
            key_block = block_of(j)
            open_ = (bits_ref[query_block, key_block] == 1) | (
                agents_ref[query_block] == agents_ref[key_block]
            )
            return (key_block < query_block) & open_

        def one_query(i, carry):
            query_block = block_of(i)
            for h in range(each):
                s = jnp.where(lower, nt(head(i, 0, h), head(i, 1, h)), -1e30)
                scores[slots, h] = s
                top[h] = s

            def score(j, carry):
                @pl.when(sees(query_block, j))
                def _():
                    for h in range(each):
                        s = nt(head(i, 0, h), head(j, 1, h))
                        scores[j, h] = s
                        top[h] = jnp.maximum(top[h], s)

                return carry

            lax.fori_loop(0, slots, score, 0)
            for h in range(each):
                summit = jnp.max(top[h], axis=1, keepdims=True)
                top[h] = jnp.broadcast_to(summit, (rows, rows))
                p = jnp.exp2((scores[slots, h] - summit) * scale)
                total[h] = p
                mixed[h] = nn(p.astype(jnp.bfloat16), head(i, 2, h))

            def weigh(j, carry):
                @pl.when(sees(query_block, j))
                def _():
                    for h in range(each):
                        p = jnp.exp2((scores[j, h] - top[h]) * scale)
                        total[h] += p
                        mixed[h] += nn(p.astype(jnp.bfloat16), head(j, 2, h))

                return carry

            lax.fori_loop(0, slots, weigh, 0)
            for h in range(each):
                sums = jnp.sum(total[h], axis=1, keepdims=True)
                done[i, h] = (mixed[h] / sums).astype(jnp.bfloat16)
            return carry

        lax.fori_loop(0, chips, one_query, 0)
        for m in range(chips):
            for h in range(each):
                outs[m][span_of(h, rows)] = done[m, h]
            if extra:
                outs[m][each * rows :] = jnp.zeros((extra, width), jnp.bfloat16)

    pairs = chips * slots // 2
    return pl.pallas_call(
        kernel,
        out_shape=[shape((each * rows + extra, width), jnp.bfloat16)] * chips,
        in_specs=[SMEM, SMEM, SMEM] + [ANY] * slots,
        out_specs=[VMEM] * chips,
        scratch_shapes=[
            pltpu.VMEM((slots, sent, width), jnp.bfloat16),
            pltpu.VMEM((slots + 1, each, rows, rows), jnp.float32),
            pltpu.VMEM((each, rows, rows), jnp.float32),
            pltpu.VMEM((each, rows, rows), jnp.float32),
            pltpu.VMEM((each, rows, width), jnp.float32),
            pltpu.VMEM((chips, each, rows, width), jnp.bfloat16),
            pltpu.SemaphoreType.DMA((slots,)),
        ],
        compiler_params=params(24),
        cost_estimate=cost(
            4 * pairs * each * rows * rows * width,
            2 * (3 * slots + chips) * each * rows * width,
            pairs * each * rows * rows,
        ),
        name="attend",
    )(place, bits, agents, *own, *other)


def unpack(place, pieces, heads, rows, each):
    chips, parts = len(pieces), len(pieces[0])
    width = pieces[0][0].shape[-1]

    def kernel(place_ref, *rest):
        ins, out_ref, turned = rest[:-2], rest[-2], rest[-1]
        chip = place_ref[0] // PAIR
        for m in range(chips):
            for part in range(parts):
                first = (chip ^ m) * (each * parts) + part * each
                for h in range(each):
                    turned[first + h] = ins[m * parts + part][span_of(h, rows)]
        for at, step in turns(heads):
            out_ref[:, at : at + step, :] = jnp.swapaxes(turned[at : at + step], 0, 1)

    return pl.pallas_call(
        kernel,
        out_shape=shape((rows, heads, width), jnp.bfloat16),
        in_specs=[SMEM] + [VMEM] * (chips * parts),
        out_specs=VMEM,
        scratch_shapes=[pltpu.VMEM((heads, rows, width), jnp.bfloat16)],
        compiler_params=params(16),
        cost_estimate=cost(0, 4 * rows * heads * width),
        name="unpack",
    )(place, *[piece for row in pieces for piece in row])


def decay_sums(decay_ref):
    decay = decay_ref[...]
    lower = triangle(decay.shape[0]).astype(jnp.bfloat16)
    return nn(lower, decay), lax.dot_general(
        decay, lower, (((0,), (1,)), ((), ())), preferred_element_type=jnp.float32
    )


def block_state(keys, values, decay):
    rows, heads, width = keys.shape

    def kernel(k_ref, v_ref, decay_ref, out_ref):
        cumul, _ = decay_sums(decay_ref)
        last = cumul[rows - 1 : rows, :]
        left = jnp.exp(last - cumul)
        for at, step in turns(heads):
            k = jnp.swapaxes(k_ref[:, at : at + step, :], 0, 1)
            v = jnp.swapaxes(v_ref[:, at : at + step, :], 0, 1)
            for h in range(step):
                kept = k[h].astype(jnp.float32) * left[:, at + h : at + h + 1]
                out_ref[at + h] = tn(kept.astype(jnp.bfloat16), v[h])
        out_ref[heads] = jnp.zeros((width, width), jnp.float32)
        out_ref[heads, 0:1, 0:heads] = last

    return pl.pallas_call(
        kernel,
        out_shape=shape((heads + 1, width, width), jnp.float32),
        in_specs=[VMEM] * 3,
        out_specs=VMEM,
        compiler_params=params(24),
        cost_estimate=cost(2 * heads * rows * width * width, 8 * rows * heads * width),
        name="block_state",
    )(keys, values, decay)


def within(queries, keys, values, decay):
    rows, heads, width = queries.shape

    def kernel(q_ref, k_ref, v_ref, decay_ref, out_ref):
        cumul, cumul_row = decay_sums(decay_ref)
        lower = triangle(rows)
        for at, step in turns(heads):
            q = jnp.swapaxes(q_ref[:, at : at + step, :], 0, 1)
            k = jnp.swapaxes(k_ref[:, at : at + step, :], 0, 1)
            v = jnp.swapaxes(v_ref[:, at : at + step, :], 0, 1)
            for h in range(step):
                i = at + h
                apart = cumul[:, i : i + 1] - cumul_row[i : i + 1, :]
                damping = jnp.where(lower, jnp.exp(jnp.where(lower, apart, 0.0)), 0.0)
                weights = (nt(q[h], k[h]) * damping).astype(jnp.bfloat16)
                out_ref[i] = nn(weights, v[h])

    return pl.pallas_call(
        kernel,
        out_shape=shape((heads, rows, width), jnp.float32),
        in_specs=[VMEM] * 4,
        out_specs=VMEM,
        compiler_params=params(24),
        cost_estimate=cost(4 * heads * rows * rows * width, 10 * rows * heads * width, heads * rows * rows),
        name="within",
    )(queries, keys, values, decay)


def join_cores(place, own, other, payloads, at_row):
    heads, width = own.shape[0] - 1, own.shape[-1]
    chips = len(payloads)
    half = heads // PAIR
    few = half // chips
    extra = few * width + LOG_ROWS

    def kernel(place_ref, own_ref, other_ref, *rest):
        outs, totals, staged, sems = rest[chips : 2 * chips], *rest[2 * chips :]
        core, chip = place_ref[0] % PAIR, place_ref[0] // PAIR
        own_logs, other_logs = own_ref[heads, 0:1, :], other_ref[heads, 0:1, :]
        logs = own_logs + other_logs
        later = jnp.exp(jnp.where(core == 0, other_logs, own_logs))
        own_factor = jnp.where(core == 0, later, 1.0)
        other_factor = jnp.where(core == 0, 1.0, later)
        for h in range(half):
            at = core * half + h
            own_by = jnp.where(core == 0, own_factor[:, h : h + 1], own_factor[:, half + h : half + h + 1])
            other_by = jnp.where(
                core == 0, other_factor[:, h : h + 1], other_factor[:, half + h : half + h + 1]
            )
            totals[h] = (own_ref[at] * own_by + other_ref[at] * other_by).astype(jnp.bfloat16)
        first = logs.astype(jnp.bfloat16).astype(jnp.float32)
        second = (logs - first).astype(jnp.bfloat16).astype(jnp.float32)
        third = logs - first - second
        row = lax.broadcasted_iota(jnp.int32, (LOG_ROWS, width), 0)
        split = jnp.where(row == 0, first, jnp.where(row == 1, second, jnp.where(row == 2, third, 0.0)))
        copies = []
        for m in range(chips):
            for h in range(few):
                staged[m, span_of(h, width)] = totals[(chip ^ m) * few + h]
            staged[m, few * width :] = split.astype(jnp.bfloat16)
            copies.append(
                pltpu.make_async_copy(staged.at[m], outs[m].at[pl.ds(at_row, extra)], sems.at[m])
            )
            copies[-1].start()
        for copy in copies:
            copy.wait()

    return pl.pallas_call(
        kernel,
        out_shape=[shape(payload.shape, payload.dtype) for payload in payloads],
        in_specs=[SMEM, VMEM, VMEM] + [ANY] * chips,
        out_specs=[ANY] * chips,
        scratch_shapes=[
            pltpu.VMEM((half, width, width), jnp.bfloat16),
            pltpu.VMEM((chips, extra, width), jnp.bfloat16),
            pltpu.SemaphoreType.DMA((chips,)),
        ],
        input_output_aliases={3 + m: m for m in range(chips)},
        compiler_params=params(24),
        cost_estimate=cost(3 * half * width * width, 14 * half * width * width),
        name="join_cores",
    )(place, own, other, *payloads)


def scan_chips(place, arrived, from_row, payloads, to_row, few, heads):
    chips = len(arrived)
    width = arrived[0].shape[-1]
    half = heads // PAIR
    extra = few * width + LOG_ROWS

    def kernel(place_ref, *rest):
        ins, outs = rest[:chips], rest[2 * chips : 3 * chips]
        got, given, state, in_sems, out_sems = rest[3 * chips :]
        core, chip = place_ref[0] % PAIR, place_ref[0] // PAIR
        copies = [
            pltpu.make_async_copy(ins[m].at[pl.ds(from_row, extra)], got.at[m], in_sems.at[m])
            for m in range(chips)
        ]
        for copy in copies:
            copy.start()
        for copy in copies:
            copy.wait()
        state[...] = jnp.zeros_like(state)
        column = lax.broadcasted_iota(jnp.int32, (1, width), 1)
        first = core * half + chip * few

        def one_chip(c, carry):
            m = c ^ chip
            logs = jnp.sum(got[m, few * width :].astype(jnp.float32), axis=0, keepdims=True)
            for h in range(few):
                span = span_of(h, width)
                here = state[span]
                given[m, span] = here.astype(jnp.bfloat16)
                log = jnp.sum(jnp.where(column == first + h, logs, 0.0), axis=1, keepdims=True)
                state[span] = here * jnp.exp(log) + got[m, span].astype(jnp.float32)
            return carry

        lax.fori_loop(0, chips, one_chip, 0)
        copies = [
            pltpu.make_async_copy(given.at[m], outs[m].at[pl.ds(to_row, few * width)], out_sems.at[m])
            for m in range(chips)
        ]
        for copy in copies:
            copy.start()
        for copy in copies:
            copy.wait()

    return pl.pallas_call(
        kernel,
        out_shape=[shape(payload.shape, payload.dtype) for payload in payloads],
        in_specs=[SMEM] + [ANY] * (2 * chips),
        out_specs=[ANY] * chips,
        scratch_shapes=[
            pltpu.VMEM((chips, extra, width), jnp.bfloat16),
            pltpu.VMEM((chips, few * width, width), jnp.bfloat16),
            pltpu.VMEM((few * width, width), jnp.float32),
            pltpu.SemaphoreType.DMA((chips,)),
            pltpu.SemaphoreType.DMA((chips,)),
        ],
        input_output_aliases={1 + chips + m: m for m in range(chips)},
        compiler_params=params(24),
        cost_estimate=cost(3 * half * width * width, 8 * half * width * width),
        name="scan_chips",
    )(place, *arrived, *payloads)


def gather_entry(place, arrived, from_row, few):
    chips = len(arrived)
    width = arrived[0].shape[-1]

    def kernel(place_ref, *rest):
        ins, out_ref = rest[:chips], rest[chips]
        chip = place_ref[0] // PAIR
        for m in range(chips):
            for h in range(few):
                out_ref[(chip ^ m) * few + h] = ins[m][pl.ds(from_row + h * width, width)]

    return pl.pallas_call(
        kernel,
        out_shape=shape((chips * few, width, width), jnp.bfloat16),
        in_specs=[SMEM] + [VMEM] * chips,
        out_specs=VMEM,
        compiler_params=params(16),
        cost_estimate=cost(0, 4 * chips * few * width * width),
        name="gather_entry",
    )(place, *arrived)


def finish(place, queries, decay, gain, inner, neighbour, entry_own, entry_other):
    rows, heads, width = queries.shape
    half = heads // PAIR

    def kernel(
        place_ref, q_ref, decay_ref, gain_ref, inner_ref, near_ref, own_ref, other_ref, out_ref, mixed
    ):
        core = place_ref[0] % PAIR
        cumul, _ = decay_sums(decay_ref)
        grown = jnp.exp(cumul)
        near_logs = near_ref[heads, 0:1, :]
        far = jnp.where(core == 0, 1.0, jnp.exp(near_logs))
        near = jnp.where(core == 0, 0.0, 1.0)
        power = jnp.zeros((rows, width), jnp.float32)
        for at, step in turns(heads):
            q = jnp.swapaxes(q_ref[:, at : at + step, :], 0, 1)
            for h in range(step):
                i = at + h
                mine, theirs = own_ref[i % half], other_ref[i % half]
                chip_entry = jnp.where(core == i // half, mine, theirs).astype(jnp.float32)
                entry = chip_entry * far[:, i : i + 1] + near_ref[i] * near
                coarse = entry.astype(jnp.bfloat16)
                fine = (entry - coarse.astype(jnp.float32)).astype(jnp.bfloat16)
                brought = (nn(q[h], coarse) + nn(q[h], fine)) * grown[:, i : i + 1]
                mix = inner_ref[i] + brought
                mixed[i] = mix
                power += mix * mix
        mean = jnp.sum(power, axis=1, keepdims=True) / (heads * width)
        norm = lax.rsqrt(mean + EPSILON)
        for at, step in turns(heads):
            normed = [
                (mixed[at + h] * norm * gain_ref[at + h : at + h + 1, :]).astype(jnp.bfloat16)
                for h in range(step)
            ]
            out_ref[:, at : at + step, :] = jnp.swapaxes(jnp.stack(normed), 0, 1)

    return pl.pallas_call(
        kernel,
        out_shape=shape((rows, heads, width), jnp.bfloat16),
        in_specs=[SMEM] + [VMEM] * 7,
        out_specs=VMEM,
        scratch_shapes=[pltpu.VMEM((heads, rows, width), jnp.float32)],
        compiler_params=params(32),
        cost_estimate=cost(4 * heads * rows * width * width, 20 * rows * heads * width),
        name="finish",
    )(place, queries, decay, gain, inner, neighbour, entry_own, entry_other)


def per_device(
    lin_q, lin_k, lin_v, lin_decay, lin_gain, soft_q, soft_k, soft_v, block_bits, agent_ids
):
    count = lax.axis_size("seq")
    chips = count // PAIR
    rows, heads, width = soft_q.shape
    lin_heads = lin_q.shape[1]
    hosted = heads // chips
    parts = min(PARTS, hosted)
    each = hosted // parts
    few = lin_heads // count
    qkv_rows, out_rows = 3 * each * rows, each * rows
    place = lax.axis_index("seq").astype(jnp.int32).reshape(1)
    masks = range(1, chips)

    def exchange(value, m):
        return lax.ppermute(value, "seq", [(i, i ^ (PAIR * m)) for i in range(count)])

    def swap_cores(value):
        return lax.ppermute(value, "seq", [(i, i ^ 1) for i in range(count)])

    def after(value, *earlier):
        return lax.optimization_barrier((value, *earlier))[0]

    packed = pack(place, (soft_q, soft_k, soft_v), chips, hosted, parts, few * width + LOG_ROWS)
    own = []
    for part in range(parts - 1):
        own.append([packed[0][part]])
        for m in masks:
            outgoing = packed[m][part]
            if part > 0:
                outgoing = after(outgoing, own[part - 1][m])
            own[part].append(exchange(outgoing, m))
        own[part] = list(lax.optimization_barrier(tuple(own[part])))

    lin_decay = after(lin_decay, packed[0][0])
    state = block_state(lin_k, lin_v, lin_decay)
    near = swap_cores(state)
    payloads = join_cores(place, state, near, [packed[m][-1] for m in range(chips)], qkv_rows)
    inner = within(lin_q, lin_k, lin_v, after(lin_decay, own[0][0], payloads[0]))
    own.append([payloads[0]])
    for m in masks:
        own[-1].append(exchange(after(payloads[m], own[parts - 2][m]) if parts > 1 else payloads[m], m))

    back = [[] for _ in range(chips)]

    def give_back(values):
        for m in range(chips):
            back[m].append(exchange(values[m], m) if m else values[m])

    mixed = None
    for part in range(parts):
        if part == parts - 1 and part > 0:
            for m in masks:
                own[part][m] = after(own[part][m], inner, mixed[0])
        other = [swap_cores(block) for block in own[part]]
        if part == parts - 1 and part > 0:
            arrived = lax.optimization_barrier((*own[part], *other[:2]))[:chips]
            give_back(scan_chips(place, arrived, qkv_rows, mixed, out_rows, few, lin_heads))
        mixed = attend(
            place, block_bits, agent_ids, own[part], other, each, rows, few * width if part == 0 else 0
        )
        if parts == 1:
            mixed = scan_chips(place, own[part], qkv_rows, mixed, out_rows, few, lin_heads)
        elif 0 < part < parts - 1:
            give_back(mixed)
    if parts > 1:
        for m in masks:
            back[m][0] = after(back[m][0], mixed[0])
    give_back(mixed)

    entry = gather_entry(place, [back[m][0] for m in range(chips)], out_rows, few)
    gain = lin_gain.reshape(lin_heads, width)
    lin_out = finish(place, lin_q, lin_decay, gain, inner, near, entry, swap_cores(entry))
    back[0][-1] = after(back[0][-1], lin_out)
    soft_out = unpack(place, back, heads, rows, each)
    return (lin_out, soft_out)


def solution(mesh):
    rows = P(("dp", "seq"), None, None)
    return jax.shard_map(
        per_device,
        mesh=mesh,
        in_specs=(rows, rows, rows, P(("dp", "seq"), None), P(), rows, rows, rows, P("dp", None), P("dp")),
        out_specs=(rows, rows),
        check_vma=False,
    )
```

```python
import jax
import jax.numpy as jnp
from jax import lax
from jax.experimental import pallas as pl
from jax.experimental.pallas import tpu as pltpu
from jax.sharding import PartitionSpec as P

EPSILON = 1e-06
PAIR = 2
ABREAST = 2
EARLY = 2
PACK_MIB = 56
WEIGHT = 1 << 29
PARTS = 1
TURN = 8
LOG_ROWS = 16
LOG2E = 1.4426950408889634
VMEM = pl.BlockSpec(memory_space=pltpu.VMEM)
SMEM = pl.BlockSpec(memory_space=pltpu.SMEM)
ANY = pl.BlockSpec(memory_space=pl.ANY)


def params(mib):
    return pltpu.CompilerParams(vmem_limit_bytes=mib << 20)


def cost(weight=1):
    return pl.CostEstimate(flops=WEIGHT * weight, bytes_accessed=1, transcendentals=0)


def shape(dims, dtype):
    return jax.ShapeDtypeStruct(dims, dtype)


def turns(heads):
    step = min(TURN, heads)
    return [(at, step) for at in range(0, heads, step)]


def span_of(index, rows):
    return pl.ds(index * rows, rows)


def nt(a, b):
    return lax.dot_general(a, b, (((1,), (1,)), ((), ())), preferred_element_type=jnp.float32)


def tn(a, b):
    return lax.dot_general(a, b, (((0,), (0,)), ((), ())), preferred_element_type=jnp.float32)


def nn(a, b):
    return lax.dot_general(a, b, (((1,), (0,)), ((), ())), preferred_element_type=jnp.float32)


def triangle(size):
    rows = lax.broadcasted_iota(jnp.int32, (size, size), 0)
    cols = lax.broadcasted_iota(jnp.int32, (size, size), 1)
    return cols <= rows


def pack(place, arrays, chips, sizes):
    rows, heads, width = arrays[0].shape
    hosted = sum(sizes)
    pieces = 2
    cut = rows // pieces

    def kernel(place_ref, q_ref, k_ref, v_ref, *rest):
        outs, (landed, turned, in_sems, out_sems) = rest[:-4], rest[-4:]
        chip = place_ref[0] // PAIR
        arriving = [
            pltpu.make_async_copy(
                ref.at[pl.ds(piece * cut, cut)],
                landed.at[which, pl.ds(piece * cut, cut)],
                in_sems.at[which, piece],
            )
            for which, ref in enumerate((q_ref, k_ref, v_ref))
            for piece in range(pieces)
        ]
        for copy in arriving:
            copy.start()
        leaving = []
        for which in range(3):
            for piece in range(pieces):
                arriving[which * pieces + piece].wait()
            for at, step in turns(heads):
                block = jnp.swapaxes(landed[which, :, at : at + step, :], 0, 1)
                for h in range(step):
                    turned[which, at + h] = block[h].T if which == 1 else block[h]
            for part, each in enumerate(sizes):
                for m in range(chips):
                    first = (chip ^ m) * hosted + sum(sizes[:part])
                    leaving.append(
                        pltpu.make_async_copy(
                            turned.at[which, pl.ds(first, each)],
                            outs[part * chips + m].at[pl.ds(which * each, each)],
                            out_sems.at[len(leaving)],
                        )
                    )
                    leaving[-1].start()
        for copy in leaving:
            copy.wait()

    outs = pl.pallas_call(
        kernel,
        out_shape=[shape((3 * each, rows, width), jnp.bfloat16) for each in sizes for _ in range(chips)],
        in_specs=[SMEM, ANY, ANY, ANY],
        out_specs=[ANY] * (chips * len(sizes)),
        scratch_shapes=[
            pltpu.VMEM((3, rows, heads, width), jnp.bfloat16),
            pltpu.VMEM((3, heads, rows, width), jnp.bfloat16),
            pltpu.SemaphoreType.DMA((3, pieces)),
            pltpu.SemaphoreType.DMA((3 * chips * len(sizes),)),
        ],
        compiler_params=params(PACK_MIB),
        cost_estimate=cost(4),
        name="pack",
    )(place, *arrays)
    return [list(outs[part * chips : (part + 1) * chips]) for part in range(len(sizes))]


def attend(place, bits, agents, own, other, each):
    chips = len(own)
    _, rows, width = own[0].shape
    slots = PAIR * chips
    scale = width**-0.5 * LOG2E
    most = sum(PAIR * chip + PAIR - 1 for chip in range(chips)) + ABREAST - 1

    def kernel(place_ref, bits_ref, agents_ref, *rest):
        ins, outs = rest[:slots], rest[slots : slots + chips]
        held, scores, top, total, mixed, probs, query_of, key_of, sems = rest[slots + chips :]
        me = place_ref[0]
        chip, core = me // PAIR, me % PAIR
        spans = [(0, 3 * each)] * chips + [(each, 2 * each)] * chips
        copies = [
            pltpu.make_async_copy(ins[j].at[pl.ds(at, size)], held.at[j, pl.ds(at, size)], sems.at[j])
            for j, (at, size) in enumerate(spans)
        ]
        for copy in copies:
            copy.start()

        found = jnp.int32(0)
        for i in range(chips):
            query_block = PAIR * (chip ^ i) + core

            def list_pair(key_block, found, i=i, query_block=query_block):
                seen = (bits_ref[query_block, key_block] == 1) | (
                    agents_ref[query_block] == agents_ref[key_block]
                )
                query_of[found] = i
                key_of[found] = (chip ^ (key_block // PAIR)) + chips * ((core + key_block) & (PAIR - 1))
                return found + seen.astype(jnp.int32)

            found = lax.fori_loop(0, query_block, list_pair, found)
        for spare in range(ABREAST - 1):
            query_of[found + spare] = 0
            key_of[found + spare] = 0
        rounds = (found + ABREAST - 1) // ABREAST

        def head(j, which, h):
            return held[j, which * each + h]

        lower = triangle(rows)
        for copy in copies[:chips]:
            copy.wait()
        for i in range(chips):
            for h in range(each):
                top[i, h] = jnp.where(lower, nn(head(i, 0, h), head(i, 1, h)), -1e30)
        for i in range(chips):
            for h in range(each):
                total[i, h] = top[i, h]
        for copy in copies[chips:]:
            copy.wait()

        def score(turn, carry):
            for lane in range(ABREAST):
                at = ABREAST * turn + lane
                i, j = query_of[at], key_of[at]
                for h in range(each):
                    s = jnp.where(at < found, nn(head(i, 0, h), head(j, 1, h)), -1e30)
                    scores[at, h] = s
                    top[i, h] = jnp.maximum(top[i, h], s)
            return carry

        lax.fori_loop(0, rounds, score, 0)
        for i in range(chips):
            for h in range(each):
                top[i, h] = jnp.broadcast_to(jnp.max(top[i, h], axis=1, keepdims=True), (rows, rows))
        for i in range(chips):
            for h in range(each):
                p = jnp.exp2((total[i, h] - top[i, h]) * scale)
                total[i, h] = p
                probs[i, h] = p.astype(jnp.bfloat16)
        for i in range(chips):
            for h in range(each):
                mixed[i, h] = nn(probs[i, h], head(i, 2, h))

        def weigh(turn, carry):
            for lane in range(ABREAST):
                at = ABREAST * turn + lane
                i = query_of[at]
                for h in range(each):
                    p = jnp.exp2((scores[at, h] - top[i, h]) * scale)
                    total[i, h] += p
                    probs[lane, h] = p.astype(jnp.bfloat16)
            for lane in range(ABREAST):
                at = ABREAST * turn + lane
                i, j = query_of[at], key_of[at]
                for h in range(each):
                    mixed[i, h] += nn(probs[lane, h], head(j, 2, h))
            return carry

        lax.fori_loop(0, rounds, weigh, 0)
        for i in range(chips):
            for h in range(each):
                sums = jnp.sum(total[i, h], axis=1, keepdims=True)
                outs[i][span_of(h, rows)] = (mixed[i, h] / sums).astype(jnp.bfloat16)

    block = (chips, each, rows, rows)
    held_bytes = 2 * each * rows * (3 * slots * width + (chips + max(chips, ABREAST)) * rows)
    score_bytes = 4 * each * rows * ((most + 2 * chips) * rows + chips * width)
    return pl.pallas_call(
        kernel,
        out_shape=[shape((each * rows, width), jnp.bfloat16)] * chips,
        in_specs=[SMEM, SMEM, SMEM] + [ANY] * slots,
        out_specs=[VMEM] * chips,
        scratch_shapes=[
            pltpu.VMEM((slots, 3 * each, rows, width), jnp.bfloat16),
            pltpu.VMEM((most, each, rows, rows), jnp.float32),
            pltpu.VMEM(block, jnp.float32),
            pltpu.VMEM(block, jnp.float32),
            pltpu.VMEM((chips, each, rows, width), jnp.float32),
            pltpu.VMEM((max(chips, ABREAST), each, rows, rows), jnp.bfloat16),
            pltpu.SMEM((most,), jnp.int32),
            pltpu.SMEM((most,), jnp.int32),
            pltpu.SemaphoreType.DMA((slots,)),
        ],
        compiler_params=params(8 + (held_bytes + score_bytes >> 20)),
        cost_estimate=cost(14),
        name="attend",
    )(place, bits, agents, *own, *other)


def unpack(place, pieces, heads, rows, sizes):
    chips, width = len(pieces[0]), pieces[0][0].shape[-1]

    def kernel(place_ref, *rest):
        ins, out_ref, turned = rest[:-2], rest[-2], rest[-1]
        chip = place_ref[0] // PAIR
        for part, each in enumerate(sizes):
            for m in range(chips):
                first = (chip ^ m) * sum(sizes) + sum(sizes[:part])
                for h in range(each):
                    turned[first + h] = ins[part * chips + m][span_of(h, rows)]
        for at, step in turns(heads):
            out_ref[:, at : at + step, :] = jnp.swapaxes(turned[at : at + step], 0, 1)

    return pl.pallas_call(
        kernel,
        out_shape=shape((rows, heads, width), jnp.bfloat16),
        in_specs=[SMEM] + [VMEM] * (chips * len(sizes)),
        out_specs=VMEM,
        scratch_shapes=[pltpu.VMEM((heads, rows, width), jnp.bfloat16)],
        compiler_params=params(16),
        cost_estimate=cost(4),
        name="unpack",
    )(place, *[piece for part in pieces for piece in part])


def decay_sums(decay_ref):
    decay = decay_ref[...]
    lower = triangle(decay.shape[0]).astype(jnp.bfloat16)
    return nn(lower, decay), lax.dot_general(
        decay, lower, (((0,), (1,)), ((), ())), preferred_element_type=jnp.float32
    )


def block_state(keys, values, decay):
    rows, heads, width = keys.shape

    def kernel(k_ref, v_ref, decay_ref, out_ref):
        cumul, _ = decay_sums(decay_ref)
        last = cumul[rows - 1 : rows, :]
        left = jnp.exp(last - cumul)
        for at, step in turns(heads):
            k = jnp.swapaxes(k_ref[:, at : at + step, :], 0, 1)
            v = jnp.swapaxes(v_ref[:, at : at + step, :], 0, 1)
            for h in range(step):
                kept = k[h].astype(jnp.float32) * left[:, at + h : at + h + 1]
                out_ref[at + h] = tn(kept.astype(jnp.bfloat16), v[h])
        out_ref[heads] = jnp.zeros((width, width), jnp.float32)
        out_ref[heads, 0:1, 0:heads] = last

    return pl.pallas_call(
        kernel,
        out_shape=shape((heads + 1, width, width), jnp.float32),
        in_specs=[VMEM] * 3,
        out_specs=VMEM,
        compiler_params=params(24),
        cost_estimate=cost(4),
        name="block_state",
    )(keys, values, decay)


def within(queries, keys, values, decay):
    rows, heads, width = queries.shape

    def kernel(q_ref, k_ref, v_ref, decay_ref, out_ref):
        cumul, cumul_row = decay_sums(decay_ref)
        lower = triangle(rows)
        for at, step in turns(heads):
            q = jnp.swapaxes(q_ref[:, at : at + step, :], 0, 1)
            k = jnp.swapaxes(k_ref[:, at : at + step, :], 0, 1)
            v = jnp.swapaxes(v_ref[:, at : at + step, :], 0, 1)
            for h in range(step):
                i = at + h
                apart = cumul[:, i : i + 1] - cumul_row[i : i + 1, :]
                damping = jnp.where(lower, jnp.exp(jnp.where(lower, apart, 0.0)), 0.0)
                weights = (nt(q[h], k[h]) * damping).astype(jnp.bfloat16)
                out_ref[i] = nn(weights, v[h])

    return pl.pallas_call(
        kernel,
        out_shape=shape((heads, rows, width), jnp.float32),
        in_specs=[VMEM] * 4,
        out_specs=VMEM,
        compiler_params=params(24),
        cost_estimate=cost(10),
        name="within",
    )(queries, keys, values, decay)


def join_cores(place, own, other, chips):
    heads, width = own.shape[0] - 1, own.shape[-1]
    half = heads // PAIR
    few = half // chips

    def kernel(place_ref, own_ref, other_ref, *rest):
        outs, totals = rest[:-1], rest[-1]
        core, chip = place_ref[0] % PAIR, place_ref[0] // PAIR
        own_logs, other_logs = own_ref[heads, 0:1, :], other_ref[heads, 0:1, :]
        logs = own_logs + other_logs
        later = jnp.exp(jnp.where(core == 0, other_logs, own_logs))
        own_factor = jnp.where(core == 0, later, 1.0)
        other_factor = jnp.where(core == 0, 1.0, later)
        for h in range(half):
            at = core * half + h
            own_by = jnp.where(core == 0, own_factor[:, h : h + 1], own_factor[:, half + h : half + h + 1])
            other_by = jnp.where(
                core == 0, other_factor[:, h : h + 1], other_factor[:, half + h : half + h + 1]
            )
            totals[h] = (own_ref[at] * own_by + other_ref[at] * other_by).astype(jnp.bfloat16)
        first = logs.astype(jnp.bfloat16).astype(jnp.float32)
        second = (logs - first).astype(jnp.bfloat16).astype(jnp.float32)
        third = logs - first - second
        row = lax.broadcasted_iota(jnp.int32, (LOG_ROWS, width), 0)
        split = jnp.where(row == 0, first, jnp.where(row == 1, second, jnp.where(row == 2, third, 0.0)))
        for m in range(chips):
            for h in range(few):
                outs[m][span_of(h, width)] = totals[(chip ^ m) * few + h]
            outs[m][few * width :] = split.astype(jnp.bfloat16)

    return pl.pallas_call(
        kernel,
        out_shape=[shape((few * width + LOG_ROWS, width), jnp.bfloat16)] * chips,
        in_specs=[SMEM, VMEM, VMEM],
        out_specs=[VMEM] * chips,
        scratch_shapes=[pltpu.VMEM((half, width, width), jnp.bfloat16)],
        compiler_params=params(24),
        cost_estimate=cost(3),
        name="join_cores",
    )(place, own, other)


def scan_chips(place, arrived, heads):
    chips = len(arrived)
    width = arrived[0].shape[-1]
    half = heads // PAIR
    few = half // chips

    def kernel(place_ref, *rest):
        ins, outs = rest[:chips], rest[chips : 2 * chips]
        got, given, state = rest[2 * chips :]
        core, chip = place_ref[0] % PAIR, place_ref[0] // PAIR
        for m in range(chips):
            got[m] = ins[m][...]
        state[...] = jnp.zeros_like(state)
        column = lax.broadcasted_iota(jnp.int32, (1, width), 1)
        first = core * half + chip * few

        def one_chip(c, carry):
            m = c ^ chip
            logs = jnp.sum(got[m, few * width :].astype(jnp.float32), axis=0, keepdims=True)
            for h in range(few):
                span = span_of(h, width)
                here = state[span]
                given[m, span] = here.astype(jnp.bfloat16)
                log = jnp.sum(jnp.where(column == first + h, logs, 0.0), axis=1, keepdims=True)
                state[span] = here * jnp.exp(log) + got[m, span].astype(jnp.float32)
            return carry

        lax.fori_loop(0, chips, one_chip, 0)
        for m in range(chips):
            outs[m][...] = given[m]

    return pl.pallas_call(
        kernel,
        out_shape=[shape((few * width, width), jnp.bfloat16)] * chips,
        in_specs=[SMEM] + [VMEM] * chips,
        out_specs=[VMEM] * chips,
        scratch_shapes=[
            pltpu.VMEM((chips, few * width + LOG_ROWS, width), jnp.bfloat16),
            pltpu.VMEM((chips, few * width, width), jnp.bfloat16),
            pltpu.VMEM((few * width, width), jnp.float32),
        ],
        compiler_params=params(24),
        cost_estimate=cost(2),
        name="scan_chips",
    )(place, *arrived)


def gather_entry(place, arrived):
    chips = len(arrived)
    width = arrived[0].shape[-1]
    few = arrived[0].shape[0] // width

    def kernel(place_ref, *rest):
        ins, out_ref = rest[:chips], rest[chips]
        chip = place_ref[0] // PAIR
        for m in range(chips):
            for h in range(few):
                out_ref[(chip ^ m) * few + h] = ins[m][span_of(h, width)]

    return pl.pallas_call(
        kernel,
        out_shape=shape((chips * few, width, width), jnp.bfloat16),
        in_specs=[SMEM] + [VMEM] * chips,
        out_specs=VMEM,
        compiler_params=params(16),
        cost_estimate=cost(1),
        name="gather_entry",
    )(place, *arrived)


def finish(place, queries, decay, gain, inner, neighbour, entry_own, entry_other):
    rows, heads, width = queries.shape
    half = heads // PAIR

    def kernel(
        place_ref, q_ref, decay_ref, gain_ref, inner_ref, near_ref, own_ref, other_ref, out_ref, mixed
    ):
        core = place_ref[0] % PAIR
        cumul, _ = decay_sums(decay_ref)
        grown = jnp.exp(cumul)
        near_logs = near_ref[heads, 0:1, :]
        far = jnp.where(core == 0, 1.0, jnp.exp(near_logs))
        near = jnp.where(core == 0, 0.0, 1.0)
        power = jnp.zeros((rows, width), jnp.float32)
        for at, step in turns(heads):
            q = jnp.swapaxes(q_ref[:, at : at + step, :], 0, 1)
            for h in range(step):
                i = at + h
                mine, theirs = own_ref[i % half], other_ref[i % half]
                chip_entry = jnp.where(core == i // half, mine, theirs).astype(jnp.float32)
                entry = chip_entry * far[:, i : i + 1] + near_ref[i] * near
                coarse = entry.astype(jnp.bfloat16)
                fine = (entry - coarse.astype(jnp.float32)).astype(jnp.bfloat16)
                brought = (nn(q[h], coarse) + nn(q[h], fine)) * grown[:, i : i + 1]
                mix = inner_ref[i] + brought
                mixed[i] = mix
                power += mix * mix
        mean = jnp.sum(power, axis=1, keepdims=True) / (heads * width)
        norm = lax.rsqrt(mean + EPSILON)
        for at, step in turns(heads):
            normed = [
                (mixed[at + h] * norm * gain_ref[at + h : at + h + 1, :]).astype(jnp.bfloat16)
                for h in range(step)
            ]
            out_ref[:, at : at + step, :] = jnp.swapaxes(jnp.stack(normed), 0, 1)

    return pl.pallas_call(
        kernel,
        out_shape=shape((rows, heads, width), jnp.bfloat16),
        in_specs=[SMEM] + [VMEM] * 7,
        out_specs=VMEM,
        scratch_shapes=[pltpu.VMEM((heads, rows, width), jnp.float32)],
        compiler_params=params(32),
        cost_estimate=cost(8),
        name="finish",
    )(place, queries, decay, gain, inner, neighbour, entry_own, entry_other)


def per_device(
    lin_q, lin_k, lin_v, lin_decay, lin_gain, soft_q, soft_k, soft_v, block_bits, agent_ids
):
    count = lax.axis_size("seq")
    chips = count // PAIR
    rows, heads, width = soft_q.shape
    lin_heads = lin_q.shape[1]
    hosted = heads // chips
    parts = min(PARTS, hosted)
    sizes = [hosted // parts] * parts
    place = lax.axis_index("seq").astype(jnp.int32).reshape(1)
    masks = range(1, chips)

    def exchange(value, m):
        return lax.ppermute(value, "seq", [(i, i ^ (PAIR * m)) for i in range(count)])

    def exchange_all(values):
        return [values[0]] + [exchange(values[m], m) for m in masks]

    def swap_cores(value):
        return lax.ppermute(value, "seq", [(i, i ^ 1) for i in range(count)])

    def after(value, *earlier):
        return lax.optimization_barrier((value, *earlier))[0]

    def together(values):
        return list(lax.optimization_barrier(tuple(values)))

    (packed,) = pack(place, (soft_q, soft_k, soft_v), chips, sizes)
    own = exchange_all(packed)
    across = swap_cores(own[0])
    decay = after(lin_decay, packed[0])
    state = block_state(lin_k, lin_v, decay)
    near = swap_cores(state)
    inner = within(lin_q, lin_k, lin_v, after(decay, state))
    totals = exchange_all(join_cores(place, state, after(near, inner, across), chips))
    arrived = together([*own, *totals])
    own, totals = arrived[:chips], arrived[chips:]
    other = [across] + [swap_cores(block) for block in own[1:]]
    starts = scan_chips(place, totals, lin_heads)

    entries = exchange_all(starts)
    mixed = attend(place, block_bits, agent_ids, own, other, hosted)
    back = [exchange_all(mixed)]
    entry = gather_entry(place, [after(block, mixed[0]) for block in entries])
    gain = lin_gain.reshape(lin_heads, width)
    lin_out = finish(place, lin_q, lin_decay, gain, inner, near, entry, swap_cores(entry))
    back[-1][0] = after(back[-1][0], lin_out)
    soft_out = unpack(place, back, heads, rows, sizes)
    return (lin_out, soft_out)


def solution(mesh):
    rows = P(("dp", "seq"), None, None)
    return jax.shard_map(
        per_device,
        mesh=mesh,
        in_specs=(rows, rows, rows, P(("dp", "seq"), None), P(), rows, rows, rows, P("dp", None), P("dp")),
        out_specs=(rows, rows),
        check_vma=False,
    )
```

```python
import jax
import jax.numpy as jnp
from jax import lax
from jax.experimental import pallas as pl
from jax.experimental.pallas import tpu as pltpu
from jax.sharding import PartitionSpec as P

EPSILON = 1e-06
PAIR = 2
ABREAST = 2
WEIGHT = 1 << 29
TURN = 8
LOG_ROWS = 16
LOG2E = 1.4426950408889634
VMEM = pl.BlockSpec(memory_space=pltpu.VMEM)
SMEM = pl.BlockSpec(memory_space=pltpu.SMEM)
ANY = pl.BlockSpec(memory_space=pl.ANY)
HBM = pl.BlockSpec(memory_space=pltpu.HBM)


def params(mib):
    return pltpu.CompilerParams(vmem_limit_bytes=mib << 20)


def cost(weight=1):
    return pl.CostEstimate(flops=WEIGHT * weight, bytes_accessed=1, transcendentals=0)


def shape(dims, dtype):
    return jax.ShapeDtypeStruct(dims, dtype)


def turns(heads):
    step = min(TURN, heads)
    return [(at, step) for at in range(0, heads, step)]


def span_of(index, rows):
    return pl.ds(index * rows, rows)


def nt(a, b):
    return lax.dot_general(a, b, (((1,), (1,)), ((), ())), preferred_element_type=jnp.float32)


def tn(a, b):
    return lax.dot_general(a, b, (((0,), (0,)), ((), ())), preferred_element_type=jnp.float32)


def nn(a, b):
    return lax.dot_general(a, b, (((1,), (0,)), ((), ())), preferred_element_type=jnp.float32)


def triangle(size):
    rows = lax.broadcasted_iota(jnp.int32, (size, size), 0)
    cols = lax.broadcasted_iota(jnp.int32, (size, size), 1)
    return cols <= rows


def pack(place, arrays, decay, chips):
    rows, heads, width = arrays[0].shape
    hosted, lin_heads = heads // chips, decay.shape[0]
    pieces = 2
    cut = rows // pieces

    def kernel(place_ref, decay_ref, q_ref, k_ref, v_ref, *rest):
        outs, (landed, turned, padded, in_sems, out_sems) = rest[:-5], rest[-5:]
        chip = place_ref[0] // PAIR
        arriving = [
            pltpu.make_async_copy(
                ref.at[pl.ds(piece * cut, cut)],
                landed.at[which, pl.ds(piece * cut, cut)],
                in_sems.at[which, piece],
            )
            for which, ref in enumerate((q_ref, k_ref, v_ref))
            for piece in range(pieces)
        ]
        for copy in arriving:
            copy.start()
        padded[...] = jnp.zeros_like(padded)
        padded[0, 0:lin_heads, :] = decay_ref[...]
        leaving = [
            pltpu.make_async_copy(padded, outs[0].at[pl.ds(3 * hosted, 1)], out_sems.at[3 * chips])
        ]
        leaving[-1].start()
        for which in range(3):
            for piece in range(pieces):
                arriving[which * pieces + piece].wait()
            for at, step in turns(heads):
                block = jnp.swapaxes(landed[which, :, at : at + step, :], 0, 1)
                for h in range(step):
                    turned[which, at + h] = block[h].T if which == 1 else block[h]
            for m in range(chips):
                leaving.append(
                    pltpu.make_async_copy(
                        turned.at[which, pl.ds((chip ^ m) * hosted, hosted)],
                        outs[m].at[pl.ds(which * hosted, hosted)],
                        out_sems.at[which * chips + m],
                    )
                )
                leaving[-1].start()
        for copy in leaving:
            copy.wait()

    return pl.pallas_call(
        kernel,
        out_shape=[shape((3 * hosted + (m == 0), rows, width), jnp.bfloat16) for m in range(chips)],
        in_specs=[SMEM, VMEM, ANY, ANY, ANY],
        out_specs=[ANY] * chips,
        scratch_shapes=[
            pltpu.VMEM((3, rows, heads, width), jnp.bfloat16),
            pltpu.VMEM((3, heads, rows, width), jnp.bfloat16),
            pltpu.VMEM((1, rows, width), jnp.bfloat16),
            pltpu.SemaphoreType.DMA((3, pieces)),
            pltpu.SemaphoreType.DMA((3 * chips + 1,)),
        ],
        compiler_params=params(56),
        cost_estimate=cost(4),
        name="pack",
    )(place, decay, *arrays)


def attend(place, bits, agents, own, other, each):
    chips = len(own)
    _, rows, width = own[0].shape
    slots = PAIR * chips
    scale = width**-0.5 * LOG2E
    most = sum(PAIR * chip + PAIR - 1 for chip in range(chips)) + ABREAST - 1

    def kernel(place_ref, bits_ref, agents_ref, *rest):
        ins, outs = rest[:slots], rest[slots : slots + chips]
        held, scores, top, total, mixed, probs, query_of, key_of, sems = rest[slots + chips :]
        me = place_ref[0]
        chip, core = me // PAIR, me % PAIR
        spans = [(0, 3 * each)] * chips + [(each, 2 * each)] * chips
        copies = [
            pltpu.make_async_copy(ins[j].at[pl.ds(at, size)], held.at[j, pl.ds(at, size)], sems.at[j])
            for j, (at, size) in enumerate(spans)
        ]
        for copy in copies[:chips]:
            copy.start()

        found = jnp.int32(0)
        for i in range(chips):
            query_block = PAIR * (chip ^ i) + core

            def list_pair(key_block, found, i=i, query_block=query_block):
                seen = (bits_ref[query_block, key_block] == 1) | (
                    agents_ref[query_block] == agents_ref[key_block]
                )
                query_of[found] = i
                key_of[found] = (chip ^ (key_block // PAIR)) + chips * ((core + key_block) & (PAIR - 1))
                return found + seen.astype(jnp.int32)

            found = lax.fori_loop(0, query_block, list_pair, found)
        for spare in range(ABREAST - 1):
            query_of[found + spare] = 0
            key_of[found + spare] = 0
        rounds = (found + ABREAST - 1) // ABREAST

        def head(j, which, h):
            return held[j, which * each + h]

        lower = triangle(rows)
        for copy in copies[:chips]:
            copy.wait()
        for copy in copies[chips:]:
            copy.start()
        for i in range(chips):
            for h in range(each):
                top[i, h] = jnp.where(lower, nn(head(i, 0, h), head(i, 1, h)), -1e30)
        for i in range(chips):
            for h in range(each):
                total[i, h] = top[i, h]
        for copy in copies[chips:]:
            copy.wait()

        def score(turn, carry):
            for lane in range(ABREAST):
                at = ABREAST * turn + lane
                i, j = query_of[at], key_of[at]
                for h in range(each):
                    s = jnp.where(at < found, nn(head(i, 0, h), head(j, 1, h)), -1e30)
                    scores[at, h] = s
                    top[i, h] = jnp.maximum(top[i, h], s)
            return carry

        lax.fori_loop(0, rounds, score, 0)
        for i in range(chips):
            for h in range(each):
                top[i, h] = jnp.broadcast_to(jnp.max(top[i, h], axis=1, keepdims=True), (rows, rows))
        for i in range(chips):
            for h in range(each):
                p = jnp.exp2((total[i, h] - top[i, h]) * scale)
                total[i, h] = p
                probs[i, h] = p.astype(jnp.bfloat16)
        for i in range(chips):
            for h in range(each):
                mixed[i, h] = nn(probs[i, h], head(i, 2, h))

        def weigh(turn, carry):
            for lane in range(ABREAST):
                at = ABREAST * turn + lane
                i = query_of[at]
                for h in range(each):
                    p = jnp.exp2((scores[at, h] - top[i, h]) * scale)
                    total[i, h] += p
                    probs[lane, h] = p.astype(jnp.bfloat16)
            for lane in range(ABREAST):
                at = ABREAST * turn + lane
                i, j = query_of[at], key_of[at]
                for h in range(each):
                    mixed[i, h] += nn(probs[lane, h], head(j, 2, h))
            return carry

        lax.fori_loop(0, rounds, weigh, 0)
        for i in range(chips):
            for h in range(each):
                sums = jnp.sum(total[i, h], axis=1, keepdims=True)
                outs[i][span_of(h, rows)] = (mixed[i, h] / sums).astype(jnp.bfloat16)

    block = (chips, each, rows, rows)
    held_bytes = 2 * each * rows * (3 * slots * width + (chips + max(chips, ABREAST)) * rows)
    score_bytes = 4 * each * rows * ((most + 2 * chips) * rows + chips * width)
    return pl.pallas_call(
        kernel,
        out_shape=[shape((each * rows, width), jnp.bfloat16)] * chips,
        in_specs=[SMEM, SMEM, SMEM] + [ANY] * slots,
        out_specs=[VMEM] * chips,
        scratch_shapes=[
            pltpu.VMEM((slots, 3 * each, rows, width), jnp.bfloat16),
            pltpu.VMEM((most, each, rows, rows), jnp.float32),
            pltpu.VMEM(block, jnp.float32),
            pltpu.VMEM(block, jnp.float32),
            pltpu.VMEM((chips, each, rows, width), jnp.float32),
            pltpu.VMEM((max(chips, ABREAST), each, rows, rows), jnp.bfloat16),
            pltpu.SMEM((most,), jnp.int32),
            pltpu.SMEM((most,), jnp.int32),
            pltpu.SemaphoreType.DMA((slots,)),
        ],
        compiler_params=params(8 + (held_bytes + score_bytes >> 20)),
        cost_estimate=cost(14),
        name="attend",
    )(place, bits, agents, *own, *other)


def unpack(place, pieces, heads, rows):
    chips, width = len(pieces), pieces[0].shape[-1]
    hosted = heads // chips

    def kernel(place_ref, *rest):
        ins, out_ref, turned = rest[:-2], rest[-2], rest[-1]
        chip = place_ref[0] // PAIR
        for m in range(chips):
            for h in range(hosted):
                turned[(chip ^ m) * hosted + h] = ins[m][span_of(h, rows)]
        for at, step in turns(heads):
            out_ref[:, at : at + step, :] = jnp.swapaxes(turned[at : at + step], 0, 1)

    return pl.pallas_call(
        kernel,
        out_shape=shape((rows, heads, width), jnp.bfloat16),
        in_specs=[SMEM] + [VMEM] * chips,
        out_specs=VMEM,
        scratch_shapes=[pltpu.VMEM((heads, rows, width), jnp.bfloat16)],
        compiler_params=params(16),
        cost_estimate=cost(4),
        name="unpack",
    )(place, *pieces)


def decay_sums(decay):
    lower = triangle(decay.shape[1]).astype(jnp.bfloat16)
    return nt(lower, decay), nt(decay, lower)


def block_state(key, value, left):
    return tn((key.astype(jnp.float32) * left).astype(jnp.bfloat16), value)


def totals_of(place, keys, values, decay, near_keys, near_values, across, chips):
    rows, heads, width = keys.shape
    half = heads // PAIR
    few = half // chips
    slot = across.shape[0] - 1

    def kernel(place_ref, k_ref, v_ref, decay_ref, near_k_ref, near_v_ref, across_ref, *rest):
        outs, (turned, near_decay, totals, sem) = rest[:chips], rest[chips:]
        core, chip = place_ref[0] % PAIR, place_ref[0] // PAIR
        copy = pltpu.make_async_copy(across_ref.at[pl.ds(slot, 1)], near_decay, sem)
        copy.start()
        for which, ref in enumerate((k_ref, v_ref, near_k_ref, near_v_ref)):
            for at, step in turns(heads):
                turned[which, at : at + step] = jnp.swapaxes(ref[:, at : at + step, :], 0, 1)
        copy.wait()
        own_sums, _ = decay_sums(decay_ref[...])
        near_sums, _ = decay_sums(near_decay[0, 0:heads, :])
        own_last, near_last = own_sums[rows - 1 : rows, :], near_sums[rows - 1 : rows, :]
        own_left = jnp.exp(own_last - own_sums)
        near_left = jnp.exp(near_last - near_sums)
        own_then = jnp.where(core == 0, jnp.exp(near_last), 1.0)
        near_then = jnp.where(core == 0, 1.0, jnp.exp(own_last))

        def half_of(sums):
            return jnp.where(core == 0, sums[:, 0:half], sums[:, half:heads])

        own_left, near_left, own_then, near_then = map(half_of, (own_left, near_left, own_then, near_then))
        for h in range(half):
            at = core * half + h
            own = block_state(turned[0, at], turned[1, at], own_left[:, h : h + 1])
            near = block_state(turned[2, at], turned[3, at], near_left[:, h : h + 1])
            total = own * own_then[:, h : h + 1] + near * near_then[:, h : h + 1]
            totals[h] = total.astype(jnp.bfloat16)
        logs = jnp.concatenate([own_last + near_last, jnp.zeros((1, width - heads), jnp.float32)], axis=1)
        first = logs.astype(jnp.bfloat16).astype(jnp.float32)
        second = (logs - first).astype(jnp.bfloat16).astype(jnp.float32)
        third = logs - first - second
        row = lax.broadcasted_iota(jnp.int32, (LOG_ROWS, width), 0)
        split = jnp.where(row == 0, first, jnp.where(row == 1, second, jnp.where(row == 2, third, 0.0)))
        for m in range(chips):
            for h in range(few):
                outs[m][span_of(h, width)] = totals[(chip ^ m) * few + h]
            outs[m][few * width :] = split.astype(jnp.bfloat16)

    return pl.pallas_call(
        kernel,
        out_shape=[shape((few * width + LOG_ROWS, width), jnp.bfloat16)] * chips,
        in_specs=[SMEM] + [VMEM] * 5 + [ANY],
        out_specs=[VMEM] * chips,
        scratch_shapes=[
            pltpu.VMEM((4, heads, rows, width), jnp.bfloat16),
            pltpu.VMEM((1, rows, width), jnp.bfloat16),
            pltpu.VMEM((half, width, width), jnp.bfloat16),
            pltpu.SemaphoreType.DMA,
        ],
        compiler_params=params(24),
        cost_estimate=cost(6),
        name="totals_of",
    )(place, keys, values, decay, near_keys, near_values, across)


def within(place, queries, keys, values, decay, near_keys, near_values, across):
    rows, heads, width = queries.shape
    slot = across.shape[0] - 1

    def kernel(place_ref, q_ref, k_ref, v_ref, decay_ref, near_k_ref, near_v_ref, across_ref, out_ref, near_decay, sem):
        core = place_ref[0] % PAIR
        copy = pltpu.make_async_copy(across_ref.at[pl.ds(slot, 1)], near_decay, sem)
        copy.start()
        cumul, cumul_row = decay_sums(decay_ref[...])
        grown = jnp.exp(cumul)
        lower = triangle(rows)
        for at, step in turns(heads):
            q = jnp.swapaxes(q_ref[:, at : at + step, :], 0, 1)
            k = jnp.swapaxes(k_ref[:, at : at + step, :], 0, 1)
            v = jnp.swapaxes(v_ref[:, at : at + step, :], 0, 1)
            for h in range(step):
                i = at + h
                apart = cumul[:, i : i + 1] - cumul_row[i : i + 1, :]
                damping = jnp.where(lower, jnp.exp(jnp.where(lower, apart, 0.0)), 0.0)
                weights = (nt(q[h], k[h]) * damping).astype(jnp.bfloat16)
                out_ref[i] = nn(weights, v[h])
        copy.wait()

        @pl.when(core > 0)
        def _():
            near_sums, _ = decay_sums(near_decay[0, 0:heads, :])
            left = jnp.exp(near_sums[rows - 1 : rows, :] - near_sums)
            for at, step in turns(heads):
                q = jnp.swapaxes(q_ref[:, at : at + step, :], 0, 1)
                k = jnp.swapaxes(near_k_ref[:, at : at + step, :], 0, 1)
                v = jnp.swapaxes(near_v_ref[:, at : at + step, :], 0, 1)
                for h in range(step):
                    i = at + h
                    state = block_state(k[h], v[h], left[:, i : i + 1])
                    out_ref[i] += precisely(q[h], state) * grown[:, i : i + 1]

    return pl.pallas_call(
        kernel,
        out_shape=shape((heads, rows, width), jnp.float32),
        in_specs=[SMEM] + [VMEM] * 6 + [ANY],
        out_specs=VMEM,
        scratch_shapes=[pltpu.VMEM((1, rows, width), jnp.bfloat16), pltpu.SemaphoreType.DMA],
        compiler_params=params(24),
        cost_estimate=cost(14),
        name="within",
    )(place, queries, keys, values, decay, near_keys, near_values, across)


def precisely(q, state):
    coarse = state.astype(jnp.bfloat16)
    fine = (state - coarse.astype(jnp.float32)).astype(jnp.bfloat16)
    return nn(q, coarse) + nn(q, fine)


def scan_chips(place, arrived, heads):
    chips = len(arrived)
    width = arrived[0].shape[-1]
    half = heads // PAIR
    few = half // chips

    def kernel(place_ref, *rest):
        ins, outs = rest[:chips], rest[chips : 2 * chips]
        got, given, state = rest[2 * chips :]
        core, chip = place_ref[0] % PAIR, place_ref[0] // PAIR
        for m in range(chips):
            got[m] = ins[m][...]
        state[...] = jnp.zeros_like(state)
        column = lax.broadcasted_iota(jnp.int32, (1, width), 1)
        first = core * half + chip * few

        def one_chip(c, carry):
            m = c ^ chip
            logs = jnp.sum(got[m, few * width :].astype(jnp.float32), axis=0, keepdims=True)
            for h in range(few):
                span = span_of(h, width)
                here = state[span]
                given[m, span] = here.astype(jnp.bfloat16)
                log = jnp.sum(jnp.where(column == first + h, logs, 0.0), axis=1, keepdims=True)
                state[span] = here * jnp.exp(log) + got[m, span].astype(jnp.float32)
            return carry

        lax.fori_loop(0, chips, one_chip, 0)
        for m in range(chips):
            outs[m][...] = given[m]

    return pl.pallas_call(
        kernel,
        out_shape=[shape((few * width, width), jnp.bfloat16)] * chips,
        in_specs=[SMEM] + [VMEM] * chips,
        out_specs=[VMEM] * chips,
        scratch_shapes=[
            pltpu.VMEM((chips, few * width + LOG_ROWS, width), jnp.bfloat16),
            pltpu.VMEM((chips, few * width, width), jnp.bfloat16),
            pltpu.VMEM((few * width, width), jnp.float32),
        ],
        compiler_params=params(24),
        cost_estimate=cost(2),
        name="scan_chips",
    )(place, *arrived)


def gather_entry(place, arrived):
    chips = len(arrived)
    width = arrived[0].shape[-1]
    few = arrived[0].shape[0] // width

    def kernel(place_ref, *rest):
        ins, out_ref = rest[:chips], rest[chips]
        chip = place_ref[0] // PAIR
        for m in range(chips):
            for h in range(few):
                out_ref[(chip ^ m) * few + h] = ins[m][span_of(h, width)]

    return pl.pallas_call(
        kernel,
        out_shape=shape((chips * few, width, width), jnp.bfloat16),
        in_specs=[SMEM] + [VMEM] * chips,
        out_specs=VMEM,
        compiler_params=params(16),
        cost_estimate=cost(1),
        name="gather_entry",
    )(place, *arrived)


def finish(place, queries, decay, across, gain, inner, entry_own, entry_other):
    rows, heads, width = queries.shape
    half = heads // PAIR
    slot = across.shape[0] - 1

    def kernel(
        place_ref, q_ref, decay_ref, gain_ref, inner_ref, own_ref, other_ref, across_ref, out_ref, mixed, near_decay, sem
    ):
        core = place_ref[0] % PAIR
        copy = pltpu.make_async_copy(across_ref.at[pl.ds(slot, 1)], near_decay, sem)
        copy.start()
        cumul, _ = decay_sums(decay_ref[...])
        copy.wait()
        near_sums, _ = decay_sums(near_decay[0, 0:heads, :])
        grown = jnp.exp(cumul + jnp.where(core == 0, 0.0, near_sums[rows - 1 : rows, :]))
        power = jnp.zeros((rows, width), jnp.float32)
        for at, step in turns(heads):
            q = jnp.swapaxes(q_ref[:, at : at + step, :], 0, 1)
            for h in range(step):
                i = at + h
                entry = jnp.where(core == i // half, own_ref[i % half], other_ref[i % half])
                mix = inner_ref[i] + nn(q[h], entry) * grown[:, i : i + 1]
                mixed[i] = mix
                power += mix * mix
        mean = jnp.sum(power, axis=1, keepdims=True) / (heads * width)
        norm = lax.rsqrt(mean + EPSILON)
        for at, step in turns(heads):
            normed = [
                (mixed[at + h] * norm * gain_ref[at + h : at + h + 1, :]).astype(jnp.bfloat16)
                for h in range(step)
            ]
            out_ref[:, at : at + step, :] = jnp.swapaxes(jnp.stack(normed), 0, 1)

    return pl.pallas_call(
        kernel,
        out_shape=shape((rows, heads, width), jnp.bfloat16),
        in_specs=[SMEM] + [VMEM] * 6 + [ANY],
        out_specs=VMEM,
        scratch_shapes=[
            pltpu.VMEM((heads, rows, width), jnp.float32),
            pltpu.VMEM((1, rows, width), jnp.bfloat16),
            pltpu.SemaphoreType.DMA,
        ],
        compiler_params=params(32),
        cost_estimate=cost(8),
        name="finish",
    )(place, queries, decay, gain, inner, entry_own, entry_other, across)


def per_device(
    lin_q, lin_k, lin_v, lin_decay, lin_gain, soft_q, soft_k, soft_v, block_bits, agent_ids
):
    count = lax.axis_size("seq")
    chips = count // PAIR
    rows, heads, width = soft_q.shape
    lin_heads = lin_q.shape[1]
    hosted = heads // chips
    place = lax.axis_index("seq").astype(jnp.int32).reshape(1)
    masks = range(1, chips)

    def exchange(value, m):
        return lax.ppermute(value, "seq", [(i, i ^ (PAIR * m)) for i in range(count)])

    def exchange_all(values):
        return [values[0]] + [exchange(values[m], m) for m in masks]

    def swap_cores(value):
        return lax.ppermute(value, "seq", [(i, i ^ 1) for i in range(count)])

    def after(value, *earlier):
        return lax.optimization_barrier((value, *earlier))[0]

    def together(values):
        return list(lax.optimization_barrier(tuple(values)))

    lin_decay = lin_decay.T
    near_k, near_v = swap_cores(lin_k), swap_cores(lin_v)
    packed = pack(place, (soft_q, soft_k, soft_v), lin_decay, chips)
    own = exchange_all(packed)
    across = swap_cores(own[0])
    totals = exchange_all(totals_of(place, lin_k, lin_v, lin_decay, near_k, near_v, across, chips))
    inner = within(place, lin_q, lin_k, lin_v, lin_decay, near_k, near_v, after(across, totals[0]))
    arrived = together([*own, *totals, inner])
    own, totals, inner = arrived[:chips], arrived[chips:-1], arrived[-1]
    other = [across] + [swap_cores(block) for block in own[1:]]
    starts = scan_chips(place, totals, lin_heads)

    entries = exchange_all(starts)
    mixed = attend(place, block_bits, agent_ids, own, other, hosted)
    back = exchange_all(mixed)
    entry = gather_entry(place, [after(block, mixed[0]) for block in entries])
    gain = lin_gain.reshape(lin_heads, width)
    lin_out = finish(place, lin_q, lin_decay, across, gain, inner, entry, swap_cores(entry))
    back[0] = after(back[0], lin_out)
    soft_out = unpack(place, back, heads, rows)
    return (lin_out, soft_out)


def solution(mesh):
    rows = P(("dp", "seq"), None, None)
    return jax.shard_map(
        per_device,
        mesh=mesh,
        in_specs=(rows, rows, rows, P(("dp", "seq"), None), P(), rows, rows, rows, P("dp", None), P("dp")),
        out_specs=(rows, rows),
        check_vma=False,
    )
```

```python
import jax
import jax.numpy as jnp
from jax import lax
from jax.experimental import pallas as pl
from jax.experimental.pallas import tpu as pltpu
from jax.sharding import PartitionSpec as P

EPSILON = 1e-06
PAIR = 2
ABREAST = 2
WEIGHT = 1 << 29
TURN = 8
LOG_ROWS = 16
LOG2E = 1.4426950408889634
VMEM = pl.BlockSpec(memory_space=pltpu.VMEM)
SMEM = pl.BlockSpec(memory_space=pltpu.SMEM)
ANY = pl.BlockSpec(memory_space=pl.ANY)
HBM = pl.BlockSpec(memory_space=pltpu.HBM)


def params(mib):
    return pltpu.CompilerParams(vmem_limit_bytes=mib << 20)


def cost(weight=1):
    return pl.CostEstimate(flops=WEIGHT * weight, bytes_accessed=1, transcendentals=0)


def shape(dims, dtype):
    return jax.ShapeDtypeStruct(dims, dtype)


def turns(heads):
    step = min(TURN, heads)
    return [(at, step) for at in range(0, heads, step)]


def span_of(index, rows):
    return pl.ds(index * rows, rows)


def nt(a, b):
    return lax.dot_general(a, b, (((1,), (1,)), ((), ())), preferred_element_type=jnp.float32)


def tn(a, b):
    return lax.dot_general(a, b, (((0,), (0,)), ((), ())), preferred_element_type=jnp.float32)


def nn(a, b):
    return lax.dot_general(a, b, (((1,), (0,)), ((), ())), preferred_element_type=jnp.float32)


def triangle(size):
    rows = lax.broadcasted_iota(jnp.int32, (size, size), 0)
    cols = lax.broadcasted_iota(jnp.int32, (size, size), 1)
    return cols <= rows


def pack(place, arrays, decay, chips):
    rows, heads, width = arrays[0].shape
    hosted, lin_heads = heads // chips, decay.shape[0]
    pieces = 2
    cut = rows // pieces

    def kernel(place_ref, decay_ref, q_ref, k_ref, v_ref, *rest):
        outs, (landed, turned, in_sems, out_sems, decay_sem) = rest[:-5], rest[-5:]
        chip = place_ref[0] // PAIR
        order = [(1, k_ref), (0, q_ref), (2, v_ref)]
        arriving = {}
        for which, ref in order:
            for piece in range(pieces):
                span = pl.ds(piece * cut, cut)
                arriving[which, piece] = pltpu.make_async_copy(
                    ref.at[span], landed.at[which, span], in_sems.at[which, piece]
                )
                arriving[which, piece].start()
        leaving = [
            pltpu.make_async_copy(decay_ref, outs[0].at[3 * hosted, pl.ds(0, lin_heads)], decay_sem)
        ]
        leaving[-1].start()

        def send(which, piece, span):
            for m in range(chips):
                leaving.append(
                    pltpu.make_async_copy(
                        turned.at[which, pl.ds((chip ^ m) * hosted, hosted), span],
                        outs[m].at[pl.ds(which * hosted, hosted), span],
                        out_sems.at[which, piece, m],
                    )
                )
                leaving[-1].start()

        for which, _ in order:
            for piece in range(pieces):
                arriving[which, piece].wait()
                if which == 1:
                    continue
                at_rows = slice(piece * cut, (piece + 1) * cut)
                for at, step in turns(heads):
                    block = jnp.swapaxes(landed[which, at_rows, at : at + step, :], 0, 1)
                    turned[which, at : at + step, at_rows, :] = block
                send(which, piece, pl.ds(piece * cut, cut))
            if which == 1:
                for at, step in turns(heads):
                    block = jnp.swapaxes(landed[which, :, at : at + step, :], 0, 1)
                    for h in range(step):
                        turned[which, at + h] = block[h].T
                send(which, 0, pl.ds(0, rows))
        for copy in leaving:
            copy.wait()

    return pl.pallas_call(
        kernel,
        out_shape=[shape((3 * hosted + (m == 0), rows, width), jnp.bfloat16) for m in range(chips)],
        in_specs=[SMEM, ANY, ANY, ANY, ANY],
        out_specs=[ANY] * chips,
        scratch_shapes=[
            pltpu.VMEM((3, rows, heads, width), jnp.bfloat16),
            pltpu.VMEM((3, heads, rows, width), jnp.bfloat16),
            pltpu.SemaphoreType.DMA((3, pieces)),
            pltpu.SemaphoreType.DMA((3, pieces, chips)),
            pltpu.SemaphoreType.DMA,
        ],
        compiler_params=params(56),
        cost_estimate=cost(4),
        name="pack",
    )(place, decay, *arrays)


def attend(place, bits, agents, own, other, each):
    chips = len(own)
    _, rows, width = own[0].shape
    slots = PAIR * chips
    scale = width**-0.5 * LOG2E
    most = sum(PAIR * chip + PAIR - 1 for chip in range(chips)) + ABREAST - 1

    def kernel(place_ref, bits_ref, agents_ref, *rest):
        ins, outs = rest[:slots], rest[slots : slots + chips]
        held, scores, top, total, mixed, probs, query_of, key_of, sems = rest[slots + chips :]
        me = place_ref[0]
        chip, core = me // PAIR, me % PAIR
        spans = [(0, 3 * each)] * chips + [(each, 2 * each)] * chips
        copies = [
            pltpu.make_async_copy(ins[j].at[pl.ds(at, size)], held.at[j, pl.ds(at, size)], sems.at[j])
            for j, (at, size) in enumerate(spans)
        ]
        for copy in copies[:chips]:
            copy.start()

        found = jnp.int32(0)
        for i in range(chips):
            query_block = PAIR * (chip ^ i) + core

            def list_pair(key_block, found, i=i, query_block=query_block):
                seen = (bits_ref[query_block, key_block] == 1) | (
                    agents_ref[query_block] == agents_ref[key_block]
                )
                query_of[found] = i
                key_of[found] = (chip ^ (key_block // PAIR)) + chips * ((core + key_block) & (PAIR - 1))
                return found + seen.astype(jnp.int32)

            found = lax.fori_loop(0, query_block, list_pair, found)
        for spare in range(ABREAST - 1):
            query_of[found + spare] = 0
            key_of[found + spare] = 0
        rounds = (found + ABREAST - 1) // ABREAST

        def head(j, which, h):
            return held[j, which * each + h]

        lower = triangle(rows)
        for copy in copies[:chips]:
            copy.wait()
        for copy in copies[chips:]:
            copy.start()
        for i in range(chips):
            for h in range(each):
                top[i, h] = jnp.where(lower, nn(head(i, 0, h), head(i, 1, h)), -1e30)
        for i in range(chips):
            for h in range(each):
                total[i, h] = top[i, h]
        for copy in copies[chips:]:
            copy.wait()

        def score(turn, carry):
            for lane in range(ABREAST):
                at = ABREAST * turn + lane
                i, j = query_of[at], key_of[at]
                for h in range(each):
                    s = jnp.where(at < found, nn(head(i, 0, h), head(j, 1, h)), -1e30)
                    scores[at, h] = s
                    top[i, h] = jnp.maximum(top[i, h], s)
            return carry

        lax.fori_loop(0, rounds, score, 0)
        for i in range(chips):
            for h in range(each):
                top[i, h] = jnp.broadcast_to(jnp.max(top[i, h], axis=1, keepdims=True), (rows, rows))
        for i in range(chips):
            for h in range(each):
                p = jnp.exp2((total[i, h] - top[i, h]) * scale)
                total[i, h] = p
                probs[i, h] = p.astype(jnp.bfloat16)
        for i in range(chips):
            for h in range(each):
                mixed[i, h] = nn(probs[i, h], head(i, 2, h))

        def weigh(turn, carry):
            for lane in range(ABREAST):
                at = ABREAST * turn + lane
                i = query_of[at]
                for h in range(each):
                    p = jnp.exp2((scores[at, h] - top[i, h]) * scale)
                    total[i, h] += p
                    probs[lane, h] = p.astype(jnp.bfloat16)
            for lane in range(ABREAST):
                at = ABREAST * turn + lane
                i, j = query_of[at], key_of[at]
                for h in range(each):
                    mixed[i, h] += nn(probs[lane, h], head(j, 2, h))
            return carry

        lax.fori_loop(0, rounds, weigh, 0)
        for i in range(chips):
            for h in range(each):
                sums = jnp.sum(total[i, h], axis=1, keepdims=True)
                outs[i][span_of(h, rows)] = (mixed[i, h] / sums).astype(jnp.bfloat16)

    block = (chips, each, rows, rows)
    held_bytes = 2 * each * rows * (3 * slots * width + (chips + max(chips, ABREAST)) * rows)
    score_bytes = 4 * each * rows * ((most + 2 * chips) * rows + chips * width)
    return pl.pallas_call(
        kernel,
        out_shape=[shape((each * rows, width), jnp.bfloat16)] * chips,
        in_specs=[SMEM, SMEM, SMEM] + [ANY] * slots,
        out_specs=[VMEM] * chips,
        scratch_shapes=[
            pltpu.VMEM((slots, 3 * each, rows, width), jnp.bfloat16),
            pltpu.VMEM((most, each, rows, rows), jnp.float32),
            pltpu.VMEM(block, jnp.float32),
            pltpu.VMEM(block, jnp.float32),
            pltpu.VMEM((chips, each, rows, width), jnp.float32),
            pltpu.VMEM((max(chips, ABREAST), each, rows, rows), jnp.bfloat16),
            pltpu.SMEM((most,), jnp.int32),
            pltpu.SMEM((most,), jnp.int32),
            pltpu.SemaphoreType.DMA((slots,)),
        ],
        compiler_params=params(8 + (held_bytes + score_bytes >> 20)),
        cost_estimate=cost(14),
        name="attend",
    )(place, bits, agents, *own, *other)


def unpack(place, pieces, heads, rows):
    chips, width = len(pieces), pieces[0].shape[-1]
    hosted = heads // chips

    def kernel(place_ref, *rest):
        ins, out_ref, turned = rest[:-2], rest[-2], rest[-1]
        chip = place_ref[0] // PAIR
        for m in range(chips):
            for h in range(hosted):
                turned[(chip ^ m) * hosted + h] = ins[m][span_of(h, rows)]
        for at, step in turns(heads):
            out_ref[:, at : at + step, :] = jnp.swapaxes(turned[at : at + step], 0, 1)

    return pl.pallas_call(
        kernel,
        out_shape=shape((rows, heads, width), jnp.bfloat16),
        in_specs=[SMEM] + [VMEM] * chips,
        out_specs=VMEM,
        scratch_shapes=[pltpu.VMEM((heads, rows, width), jnp.bfloat16)],
        compiler_params=params(16),
        cost_estimate=cost(4),
        name="unpack",
    )(place, *pieces)


def decay_sums(decay):
    lower = triangle(decay.shape[1]).astype(jnp.bfloat16)
    return nt(lower, decay), nt(decay, lower)


def block_state(key, value, left):
    return tn((key.astype(jnp.float32) * left).astype(jnp.bfloat16), value)


def totals_of(place, keys, values, decay, near_keys, near_values, across, chips):
    rows, heads, width = keys.shape
    half = heads // PAIR
    few = half // chips
    slot = across.shape[0] - 1

    def kernel(place_ref, k_ref, v_ref, decay_ref, near_k_ref, near_v_ref, across_ref, *rest):
        outs, (turned, near_decay, totals, sem) = rest[:chips], rest[chips:]
        core, chip = place_ref[0] % PAIR, place_ref[0] // PAIR
        copy = pltpu.make_async_copy(across_ref.at[pl.ds(slot, 1)], near_decay, sem)
        copy.start()
        for which, ref in enumerate((k_ref, v_ref, near_k_ref, near_v_ref)):
            for at, step in turns(heads):
                turned[which, at : at + step] = jnp.swapaxes(ref[:, at : at + step, :], 0, 1)
        copy.wait()
        own_sums, _ = decay_sums(decay_ref[...])
        near_sums, _ = decay_sums(near_decay[0, 0:heads, :])
        own_last, near_last = own_sums[rows - 1 : rows, :], near_sums[rows - 1 : rows, :]
        own_left = jnp.exp(own_last - own_sums)
        near_left = jnp.exp(near_last - near_sums)
        own_then = jnp.where(core == 0, jnp.exp(near_last), 1.0)
        near_then = jnp.where(core == 0, 1.0, jnp.exp(own_last))

        def half_of(sums):
            return jnp.where(core == 0, sums[:, 0:half], sums[:, half:heads])

        own_left, near_left, own_then, near_then = map(half_of, (own_left, near_left, own_then, near_then))
        for h in range(half):
            at = core * half + h
            own = block_state(turned[0, at], turned[1, at], own_left[:, h : h + 1])
            near = block_state(turned[2, at], turned[3, at], near_left[:, h : h + 1])
            total = own * own_then[:, h : h + 1] + near * near_then[:, h : h + 1]
            totals[h] = total.astype(jnp.bfloat16)
        logs = jnp.concatenate([own_last + near_last, jnp.zeros((1, width - heads), jnp.float32)], axis=1)
        first = logs.astype(jnp.bfloat16).astype(jnp.float32)
        second = (logs - first).astype(jnp.bfloat16).astype(jnp.float32)
        third = logs - first - second
        row = lax.broadcasted_iota(jnp.int32, (LOG_ROWS, width), 0)
        split = jnp.where(row == 0, first, jnp.where(row == 1, second, jnp.where(row == 2, third, 0.0)))
        for m in range(chips):
            for h in range(few):
                outs[m][span_of(h, width)] = totals[(chip ^ m) * few + h]
            outs[m][few * width :] = split.astype(jnp.bfloat16)

    return pl.pallas_call(
        kernel,
        out_shape=[shape((few * width + LOG_ROWS, width), jnp.bfloat16)] * chips,
        in_specs=[SMEM] + [VMEM] * 5 + [ANY],
        out_specs=[VMEM] * chips,
        scratch_shapes=[
            pltpu.VMEM((4, heads, rows, width), jnp.bfloat16),
            pltpu.VMEM((1, rows, width), jnp.bfloat16),
            pltpu.VMEM((half, width, width), jnp.bfloat16),
            pltpu.SemaphoreType.DMA,
        ],
        compiler_params=params(24),
        cost_estimate=cost(6),
        name="totals_of",
    )(place, keys, values, decay, near_keys, near_values, across)


def within(place, queries, keys, values, decay, near_keys, near_values, across):
    rows, heads, width = queries.shape
    slot = across.shape[0] - 1

    def kernel(place_ref, q_ref, k_ref, v_ref, decay_ref, near_k_ref, near_v_ref, across_ref, out_ref, near_decay, sem):
        core = place_ref[0] % PAIR
        copy = pltpu.make_async_copy(across_ref.at[pl.ds(slot, 1)], near_decay, sem)
        copy.start()
        cumul, cumul_row = decay_sums(decay_ref[...])
        grown = jnp.exp(cumul)
        lower = triangle(rows)
        for at, step in turns(heads):
            q = jnp.swapaxes(q_ref[:, at : at + step, :], 0, 1)
            k = jnp.swapaxes(k_ref[:, at : at + step, :], 0, 1)
            v = jnp.swapaxes(v_ref[:, at : at + step, :], 0, 1)
            for h in range(step):
                i = at + h
                apart = cumul[:, i : i + 1] - cumul_row[i : i + 1, :]
                damping = jnp.where(lower, jnp.exp(jnp.where(lower, apart, 0.0)), 0.0)
                weights = (nt(q[h], k[h]) * damping).astype(jnp.bfloat16)
                out_ref[i] = nn(weights, v[h])
        copy.wait()

        @pl.when(core > 0)
        def _():
            near_sums, _ = decay_sums(near_decay[0, 0:heads, :])
            left = jnp.exp(near_sums[rows - 1 : rows, :] - near_sums)
            for at, step in turns(heads):
                q = jnp.swapaxes(q_ref[:, at : at + step, :], 0, 1)
                k = jnp.swapaxes(near_k_ref[:, at : at + step, :], 0, 1)
                v = jnp.swapaxes(near_v_ref[:, at : at + step, :], 0, 1)
                for h in range(step):
                    i = at + h
                    state = block_state(k[h], v[h], left[:, i : i + 1])
                    out_ref[i] += precisely(q[h], state) * grown[:, i : i + 1]

    return pl.pallas_call(
        kernel,
        out_shape=shape((heads, rows, width), jnp.float32),
        in_specs=[SMEM] + [VMEM] * 6 + [ANY],
        out_specs=VMEM,
        scratch_shapes=[pltpu.VMEM((1, rows, width), jnp.bfloat16), pltpu.SemaphoreType.DMA],
        compiler_params=params(24),
        cost_estimate=cost(14),
        name="within",
    )(place, queries, keys, values, decay, near_keys, near_values, across)


def precisely(q, state):
    coarse = state.astype(jnp.bfloat16)
    fine = (state - coarse.astype(jnp.float32)).astype(jnp.bfloat16)
    return nn(q, coarse) + nn(q, fine)


def scan_chips(place, arrived, heads):
    chips = len(arrived)
    width = arrived[0].shape[-1]
    half = heads // PAIR
    few = half // chips

    def kernel(place_ref, *rest):
        ins, outs = rest[:chips], rest[chips : 2 * chips]
        got, given, state = rest[2 * chips :]
        core, chip = place_ref[0] % PAIR, place_ref[0] // PAIR
        for m in range(chips):
            got[m] = ins[m][...]
        state[...] = jnp.zeros_like(state)
        column = lax.broadcasted_iota(jnp.int32, (1, width), 1)
        first = core * half + chip * few

        def one_chip(c, carry):
            m = c ^ chip
            logs = jnp.sum(got[m, few * width :].astype(jnp.float32), axis=0, keepdims=True)
            for h in range(few):
                span = span_of(h, width)
                here = state[span]
                given[m, span] = here.astype(jnp.bfloat16)
                log = jnp.sum(jnp.where(column == first + h, logs, 0.0), axis=1, keepdims=True)
                state[span] = here * jnp.exp(log) + got[m, span].astype(jnp.float32)
            return carry

        lax.fori_loop(0, chips, one_chip, 0)
        for m in range(chips):
            outs[m][...] = given[m]

    return pl.pallas_call(
        kernel,
        out_shape=[shape((few * width, width), jnp.bfloat16)] * chips,
        in_specs=[SMEM] + [VMEM] * chips,
        out_specs=[VMEM] * chips,
        scratch_shapes=[
            pltpu.VMEM((chips, few * width + LOG_ROWS, width), jnp.bfloat16),
            pltpu.VMEM((chips, few * width, width), jnp.bfloat16),
            pltpu.VMEM((few * width, width), jnp.float32),
        ],
        compiler_params=params(24),
        cost_estimate=cost(2),
        name="scan_chips",
    )(place, *arrived)


def gather_entry(place, arrived):
    chips = len(arrived)
    width = arrived[0].shape[-1]
    few = arrived[0].shape[0] // width

    def kernel(place_ref, *rest):
        ins, out_ref = rest[:chips], rest[chips]
        chip = place_ref[0] // PAIR
        for m in range(chips):
            for h in range(few):
                out_ref[(chip ^ m) * few + h] = ins[m][span_of(h, width)]

    return pl.pallas_call(
        kernel,
        out_shape=shape((chips * few, width, width), jnp.bfloat16),
        in_specs=[SMEM] + [VMEM] * chips,
        out_specs=VMEM,
        compiler_params=params(16),
        cost_estimate=cost(1),
        name="gather_entry",
    )(place, *arrived)


def finish(place, queries, decay, across, gain, inner, entry_own, entry_other):
    rows, heads, width = queries.shape
    half = heads // PAIR
    slot = across.shape[0] - 1

    def kernel(
        place_ref, q_ref, decay_ref, gain_ref, inner_ref, own_ref, other_ref, across_ref, out_ref, mixed, near_decay, sem
    ):
        core = place_ref[0] % PAIR
        copy = pltpu.make_async_copy(across_ref.at[pl.ds(slot, 1)], near_decay, sem)
        copy.start()
        cumul, _ = decay_sums(decay_ref[...])
        copy.wait()
        near_sums, _ = decay_sums(near_decay[0, 0:heads, :])
        grown = jnp.exp(cumul + jnp.where(core == 0, 0.0, near_sums[rows - 1 : rows, :]))
        power = jnp.zeros((rows, width), jnp.float32)
        for at, step in turns(heads):
            q = jnp.swapaxes(q_ref[:, at : at + step, :], 0, 1)
            for h in range(step):
                i = at + h
                entry = jnp.where(core == i // half, own_ref[i % half], other_ref[i % half])
                mix = inner_ref[i] + nn(q[h], entry) * grown[:, i : i + 1]
                mixed[i] = mix
                power += mix * mix
        mean = jnp.sum(power, axis=1, keepdims=True) / (heads * width)
        norm = lax.rsqrt(mean + EPSILON)
        for at, step in turns(heads):
            normed = [
                (mixed[at + h] * norm * gain_ref[at + h : at + h + 1, :]).astype(jnp.bfloat16)
                for h in range(step)
            ]
            out_ref[:, at : at + step, :] = jnp.swapaxes(jnp.stack(normed), 0, 1)

    return pl.pallas_call(
        kernel,
        out_shape=shape((rows, heads, width), jnp.bfloat16),
        in_specs=[SMEM] + [VMEM] * 6 + [ANY],
        out_specs=VMEM,
        scratch_shapes=[
            pltpu.VMEM((heads, rows, width), jnp.float32),
            pltpu.VMEM((1, rows, width), jnp.bfloat16),
            pltpu.SemaphoreType.DMA,
        ],
        compiler_params=params(32),
        cost_estimate=cost(8),
        name="finish",
    )(place, queries, decay, gain, inner, entry_own, entry_other, across)


def per_device(
    lin_q, lin_k, lin_v, lin_decay, lin_gain, soft_q, soft_k, soft_v, block_bits, agent_ids
):
    count = lax.axis_size("seq")
    chips = count // PAIR
    rows, heads, width = soft_q.shape
    lin_heads = lin_q.shape[1]
    hosted = heads // chips
    place = lax.axis_index("seq").astype(jnp.int32).reshape(1)
    masks = range(1, chips)

    def exchange(value, m):
        return lax.ppermute(value, "seq", [(i, i ^ (PAIR * m)) for i in range(count)])

    def exchange_all(values):
        return [values[0]] + [exchange(values[m], m) for m in masks]

    def swap_cores(value):
        return lax.ppermute(value, "seq", [(i, i ^ 1) for i in range(count)])

    def after(value, *earlier):
        return lax.optimization_barrier((value, *earlier))[0]

    def together(values):
        return list(lax.optimization_barrier(tuple(values)))

    lin_decay = lin_decay.T
    near_k, near_v = swap_cores(lin_k), swap_cores(lin_v)
    packed = pack(place, (soft_q, soft_k, soft_v), lin_decay, chips)
    across = swap_cores(packed[0])
    totals = totals_of(place, lin_k, lin_v, lin_decay, near_k, near_v, across, chips)
    own = exchange_all([*packed[:-1], after(packed[-1], totals[0])])
    totals = exchange_all(totals)
    inner = within(place, lin_q, lin_k, lin_v, lin_decay, near_k, near_v, after(across, totals[0]))
    arrived = together([*own, *totals, inner])
    own, totals, inner = arrived[:chips], arrived[chips:-1], arrived[-1]
    other = [across] + [swap_cores(block) for block in own[1:]]
    starts = scan_chips(place, totals, lin_heads)

    entries = exchange_all(starts)
    mixed = attend(place, block_bits, agent_ids, own, other, hosted)
    back = exchange_all(mixed)
    entry = gather_entry(place, [after(block, mixed[0]) for block in entries])
    gain = lin_gain.reshape(lin_heads, width)
    lin_out = finish(place, lin_q, lin_decay, across, gain, inner, entry, swap_cores(entry))
    back[0] = after(back[0], lin_out)
    soft_out = unpack(place, back, heads, rows)
    return (lin_out, soft_out)


def solution(mesh):
    rows = P(("dp", "seq"), None, None)
    return jax.shard_map(
        per_device,
        mesh=mesh,
        in_specs=(rows, rows, rows, P(("dp", "seq"), None), P(), rows, rows, rows, P("dp", None), P("dp")),
        out_specs=(rows, rows),
        check_vma=False,
    )
```

```python
import jax
import jax.numpy as jnp
from jax import lax
from jax.experimental import pallas as pl
from jax.experimental.pallas import tpu as pltpu
from jax.sharding import PartitionSpec as P

EPSILON = 1e-06
PAIR = 2
WEIGHT = 1 << 31
TURN = 8
LOG_ROWS = 16
LOG2E = 1.4426950408889634
VMEM = pl.BlockSpec(memory_space=pltpu.VMEM)
SMEM = pl.BlockSpec(memory_space=pltpu.SMEM)
ANY = pl.BlockSpec(memory_space=pl.ANY)
HBM = pl.BlockSpec(memory_space=pltpu.HBM)


def params(mib):
    return pltpu.CompilerParams(vmem_limit_bytes=mib << 20)


def cost(weight=1):
    return pl.CostEstimate(flops=WEIGHT * weight, bytes_accessed=1, transcendentals=0)


def shape(dims, dtype):
    return jax.ShapeDtypeStruct(dims, dtype)


def turns(heads):
    step = min(TURN, heads)
    return [(at, step) for at in range(0, heads, step)]


def span_of(index, rows):
    return pl.ds(index * rows, rows)


def nt(a, b):
    return lax.dot_general(a, b, (((1,), (1,)), ((), ())), preferred_element_type=jnp.float32)


def tn(a, b):
    return lax.dot_general(a, b, (((0,), (0,)), ((), ())), preferred_element_type=jnp.float32)


def nn(a, b):
    return lax.dot_general(a, b, (((1,), (0,)), ((), ())), preferred_element_type=jnp.float32)


def triangle(size):
    rows = lax.broadcasted_iota(jnp.int32, (size, size), 0)
    cols = lax.broadcasted_iota(jnp.int32, (size, size), 1)
    return cols <= rows


def pack(place, arrays, decay, chips):
    rows, heads, width = arrays[0].shape
    hosted, lin_heads = heads // chips, decay.shape[0]
    pieces = 2
    cut = rows // pieces

    def kernel(place_ref, decay_ref, q_ref, k_ref, v_ref, *rest):
        outs, (landed, turned, in_sems, out_sems, decay_sem) = rest[:-5], rest[-5:]
        chip = place_ref[0] // PAIR
        order = [(1, k_ref), (0, q_ref), (2, v_ref)]
        arriving = {}
        for which, ref in order:
            for piece in range(pieces):
                span = pl.ds(piece * cut, cut)
                arriving[which, piece] = pltpu.make_async_copy(
                    ref.at[span], landed.at[which, span], in_sems.at[which, piece]
                )
                arriving[which, piece].start()
        leaving = [
            pltpu.make_async_copy(decay_ref, outs[0].at[3 * hosted, pl.ds(0, lin_heads)], decay_sem)
        ]
        leaving[-1].start()

        def send(which, piece, span):
            for m in range(chips):
                leaving.append(
                    pltpu.make_async_copy(
                        turned.at[which, pl.ds((chip ^ m) * hosted, hosted), span],
                        outs[m].at[pl.ds(which * hosted, hosted), span],
                        out_sems.at[which, piece, m],
                    )
                )
                leaving[-1].start()

        for which, _ in order:
            for piece in range(pieces):
                arriving[which, piece].wait()
                if which == 1:
                    continue
                at_rows = slice(piece * cut, (piece + 1) * cut)
                for at, step in turns(heads):
                    block = jnp.swapaxes(landed[which, at_rows, at : at + step, :], 0, 1)
                    turned[which, at : at + step, at_rows, :] = block
                send(which, piece, pl.ds(piece * cut, cut))
            if which == 1:
                for at, step in turns(heads):
                    block = jnp.swapaxes(landed[which, :, at : at + step, :], 0, 1)
                    for h in range(step):
                        turned[which, at + h] = block[h].T
                send(which, 0, pl.ds(0, rows))
        for copy in leaving:
            copy.wait()

    return pl.pallas_call(
        kernel,
        out_shape=[shape((3 * hosted + (m == 0), rows, width), jnp.bfloat16) for m in range(chips)],
        in_specs=[SMEM, ANY, ANY, ANY, ANY],
        out_specs=[ANY] * chips,
        scratch_shapes=[
            pltpu.VMEM((3, rows, heads, width), jnp.bfloat16),
            pltpu.VMEM((3, heads, rows, width), jnp.bfloat16),
            pltpu.SemaphoreType.DMA((3, pieces)),
            pltpu.SemaphoreType.DMA((3, pieces, chips)),
            pltpu.SemaphoreType.DMA,
        ],
        compiler_params=params(56),
        cost_estimate=cost(4),
        name="pack",
    )(place, decay, *arrays)


def attend(place, bits, agents, own, other, each):
    chips = len(own)
    _, rows, width = own[0].shape
    slots = PAIR * chips
    scale = width**-0.5 * LOG2E
    most = sum(PAIR * chip + PAIR - 1 for chip in range(chips))

    def kernel(place_ref, bits_ref, agents_ref, *rest):
        ins, outs = rest[:slots], rest[slots : slots + chips]
        queries, scores, top, total, mixed, probs, query_of = rest[slots + chips :]
        me = place_ref[0]
        chip, core = me // PAIR, me % PAIR

        found, ends = jnp.int32(0), []
        for j in range(slots):
            key_block = PAIR * (chip ^ (j % chips)) + (core if j < chips else PAIR - 1 - core)

            for i in range(chips):
                query_block = PAIR * (chip ^ i) + core
                seen = (key_block < query_block) & (
                    (bits_ref[query_block, key_block] == 1) | (agents_ref[query_block] == agents_ref[key_block])
                )
                query_of[found] = i
                found = found + seen.astype(jnp.int32)
            ends.append(found)

        lower = triangle(rows)
        for i in range(chips):
            for h in range(each):
                queries[i, h] = ins[i][h]
                top[i, h] = jnp.where(lower, nn(ins[i][h], ins[i][each + h]), -1e30)
        for i in range(chips):
            for h in range(each):
                total[i, h] = top[i, h]

        for j in range(slots):

            def score(at, carry, j=j):
                i = query_of[at]
                for h in range(each):
                    s = nn(queries[i, h], ins[j][each + h])
                    scores[at, h] = s
                    top[i, h] = jnp.maximum(top[i, h], s)
                return carry

            lax.fori_loop(ends[j - 1] if j else 0, ends[j], score, 0)

        for i in range(chips):
            for h in range(each):
                top[i, h] = jnp.broadcast_to(jnp.max(top[i, h], axis=1, keepdims=True), (rows, rows))
        for i in range(chips):
            for h in range(each):
                p = jnp.exp2((total[i, h] - top[i, h]) * scale)
                total[i, h] = p
                probs[i, h] = p.astype(jnp.bfloat16)
        for i in range(chips):
            for h in range(each):
                mixed[i, h] = nn(probs[i, h], ins[i][2 * each + h])

        for j in range(slots):

            def weigh(at, carry, j=j):
                i = query_of[at]
                for h in range(each):
                    p = jnp.exp2((scores[at, h] - top[i, h]) * scale)
                    total[i, h] += p
                    probs[0, h] = p.astype(jnp.bfloat16)
                for h in range(each):
                    mixed[i, h] += nn(probs[0, h], ins[j][2 * each + h])
                return carry

            lax.fori_loop(ends[j - 1] if j else 0, ends[j], weigh, 0)

        for i in range(chips):
            for h in range(each):
                sums = jnp.sum(total[i, h], axis=1, keepdims=True)
                outs[i][span_of(h, rows)] = (mixed[i, h] / sums).astype(jnp.bfloat16)

    block = (chips, each, rows, rows)
    in_bytes = 2 * each * rows * (3 * slots * width + 3 * chips * rows)
    score_bytes = 4 * each * rows * ((most + 2 * chips) * rows + chips * width)
    return pl.pallas_call(
        kernel,
        out_shape=[shape((each * rows, width), jnp.bfloat16)] * chips,
        in_specs=[SMEM, SMEM, SMEM] + [VMEM] * slots,
        out_specs=[VMEM] * chips,
        scratch_shapes=[
            pltpu.VMEM((chips, each, rows, width), jnp.bfloat16),
            pltpu.VMEM((most, each, rows, rows), jnp.float32),
            pltpu.VMEM(block, jnp.float32),
            pltpu.VMEM(block, jnp.float32),
            pltpu.VMEM((chips, each, rows, width), jnp.float32),
            pltpu.VMEM(block, jnp.bfloat16),
            pltpu.SMEM((most + 1,), jnp.int32),
        ],
        compiler_params=params(6 + (in_bytes + score_bytes >> 20)),
        cost_estimate=cost(14),
        name="attend",
    )(place, bits, agents, *own, *other)


def unpack(place, pieces, heads, rows):
    chips, width = len(pieces), pieces[0].shape[-1]
    hosted = heads // chips

    def kernel(place_ref, *rest):
        ins, out_ref, turned = rest[:-2], rest[-2], rest[-1]
        chip = place_ref[0] // PAIR
        for m in range(chips):
            for h in range(hosted):
                turned[(chip ^ m) * hosted + h] = ins[m][span_of(h, rows)]
        for at, step in turns(heads):
            out_ref[:, at : at + step, :] = jnp.swapaxes(turned[at : at + step], 0, 1)

    return pl.pallas_call(
        kernel,
        out_shape=shape((rows, heads, width), jnp.bfloat16),
        in_specs=[SMEM] + [VMEM] * chips,
        out_specs=VMEM,
        scratch_shapes=[pltpu.VMEM((heads, rows, width), jnp.bfloat16)],
        compiler_params=params(16),
        cost_estimate=cost(4),
        name="unpack",
    )(place, *pieces)


def decay_sums(decay):
    lower = triangle(decay.shape[1]).astype(jnp.bfloat16)
    return nt(lower, decay), nt(decay, lower)


def block_state(key, value, left):
    return tn((key.astype(jnp.float32) * left).astype(jnp.bfloat16), value)


def totals_of(place, keys, values, decay, near_keys, near_values, across, chips):
    rows, heads, width = keys.shape
    half = heads // PAIR
    few = half // chips
    slot = across.shape[0] - 1

    def kernel(place_ref, k_ref, v_ref, decay_ref, near_k_ref, near_v_ref, across_ref, *rest):
        outs, (turned, near_decay, totals, sem) = rest[:chips], rest[chips:]
        core, chip = place_ref[0] % PAIR, place_ref[0] // PAIR
        copy = pltpu.make_async_copy(across_ref.at[pl.ds(slot, 1)], near_decay, sem)
        copy.start()
        for which, ref in enumerate((k_ref, v_ref, near_k_ref, near_v_ref)):
            for at, step in turns(heads):
                turned[which, at : at + step] = jnp.swapaxes(ref[:, at : at + step, :], 0, 1)
        copy.wait()
        own_sums, _ = decay_sums(decay_ref[...])
        near_sums, _ = decay_sums(near_decay[0, 0:heads, :])
        own_last, near_last = own_sums[rows - 1 : rows, :], near_sums[rows - 1 : rows, :]
        own_left = jnp.exp(own_last - own_sums)
        near_left = jnp.exp(near_last - near_sums)
        own_then = jnp.where(core == 0, jnp.exp(near_last), 1.0)
        near_then = jnp.where(core == 0, 1.0, jnp.exp(own_last))

        def half_of(sums):
            return jnp.where(core == 0, sums[:, 0:half], sums[:, half:heads])

        own_left, near_left, own_then, near_then = map(half_of, (own_left, near_left, own_then, near_then))
        for h in range(half):
            at = core * half + h
            own = block_state(turned[0, at], turned[1, at], own_left[:, h : h + 1])
            near = block_state(turned[2, at], turned[3, at], near_left[:, h : h + 1])
            total = own * own_then[:, h : h + 1] + near * near_then[:, h : h + 1]
            totals[h] = total.astype(jnp.bfloat16)
        logs = jnp.concatenate([own_last + near_last, jnp.zeros((1, width - heads), jnp.float32)], axis=1)
        first = logs.astype(jnp.bfloat16).astype(jnp.float32)
        second = (logs - first).astype(jnp.bfloat16).astype(jnp.float32)
        third = logs - first - second
        row = lax.broadcasted_iota(jnp.int32, (LOG_ROWS, width), 0)
        split = jnp.where(row == 0, first, jnp.where(row == 1, second, jnp.where(row == 2, third, 0.0)))
        for m in range(chips):
            for h in range(few):
                outs[m][span_of(h, width)] = totals[(chip ^ m) * few + h]
            outs[m][few * width :] = split.astype(jnp.bfloat16)

    return pl.pallas_call(
        kernel,
        out_shape=[shape((few * width + LOG_ROWS, width), jnp.bfloat16)] * chips,
        in_specs=[SMEM] + [VMEM] * 5 + [ANY],
        out_specs=[VMEM] * chips,
        scratch_shapes=[
            pltpu.VMEM((4, heads, rows, width), jnp.bfloat16),
            pltpu.VMEM((1, rows, width), jnp.bfloat16),
            pltpu.VMEM((half, width, width), jnp.bfloat16),
            pltpu.SemaphoreType.DMA,
        ],
        compiler_params=params(24),
        cost_estimate=cost(6),
        name="totals_of",
    )(place, keys, values, decay, near_keys, near_values, across)


def within(place, queries, keys, values, decay, near_keys, near_values, across):
    rows, heads, width = queries.shape
    slot = across.shape[0] - 1

    def kernel(place_ref, q_ref, k_ref, v_ref, decay_ref, near_k_ref, near_v_ref, across_ref, out_ref, near_decay, sem):
        core = place_ref[0] % PAIR
        copy = pltpu.make_async_copy(across_ref.at[pl.ds(slot, 1)], near_decay, sem)
        copy.start()
        cumul, cumul_row = decay_sums(decay_ref[...])
        grown = jnp.exp(cumul)
        lower = triangle(rows)
        for at, step in turns(heads):
            q = jnp.swapaxes(q_ref[:, at : at + step, :], 0, 1)
            k = jnp.swapaxes(k_ref[:, at : at + step, :], 0, 1)
            v = jnp.swapaxes(v_ref[:, at : at + step, :], 0, 1)
            for h in range(step):
                i = at + h
                apart = cumul[:, i : i + 1] - cumul_row[i : i + 1, :]
                damping = jnp.where(lower, jnp.exp(jnp.where(lower, apart, 0.0)), 0.0)
                weights = (nt(q[h], k[h]) * damping).astype(jnp.bfloat16)
                out_ref[i] = nn(weights, v[h])
        copy.wait()

        @pl.when(core > 0)
        def _():
            near_sums, _ = decay_sums(near_decay[0, 0:heads, :])
            left = jnp.exp(near_sums[rows - 1 : rows, :] - near_sums)
            for at, step in turns(heads):
                q = jnp.swapaxes(q_ref[:, at : at + step, :], 0, 1)
                k = jnp.swapaxes(near_k_ref[:, at : at + step, :], 0, 1)
                v = jnp.swapaxes(near_v_ref[:, at : at + step, :], 0, 1)
                for h in range(step):
                    i = at + h
                    state = block_state(k[h], v[h], left[:, i : i + 1])
                    out_ref[i] += precisely(q[h], state) * grown[:, i : i + 1]

    return pl.pallas_call(
        kernel,
        out_shape=shape((heads, rows, width), jnp.float32),
        in_specs=[SMEM] + [VMEM] * 6 + [ANY],
        out_specs=VMEM,
        scratch_shapes=[pltpu.VMEM((1, rows, width), jnp.bfloat16), pltpu.SemaphoreType.DMA],
        compiler_params=params(24),
        cost_estimate=cost(14),
        name="within",
    )(place, queries, keys, values, decay, near_keys, near_values, across)


def precisely(q, state):
    coarse = state.astype(jnp.bfloat16)
    fine = (state - coarse.astype(jnp.float32)).astype(jnp.bfloat16)
    return nn(q, coarse) + nn(q, fine)


def scan_chips(place, arrived, heads):
    chips = len(arrived)
    width = arrived[0].shape[-1]
    half = heads // PAIR
    few = half // chips

    def kernel(place_ref, *rest):
        ins, outs = rest[:chips], rest[chips : 2 * chips]
        got, given, state = rest[2 * chips :]
        core, chip = place_ref[0] % PAIR, place_ref[0] // PAIR
        for m in range(chips):
            got[m] = ins[m][...]
        state[...] = jnp.zeros_like(state)
        column = lax.broadcasted_iota(jnp.int32, (1, width), 1)
        first = core * half + chip * few

        def one_chip(c, carry):
            m = c ^ chip
            logs = jnp.sum(got[m, few * width :].astype(jnp.float32), axis=0, keepdims=True)
            for h in range(few):
                span = span_of(h, width)
                here = state[span]
                given[m, span] = here.astype(jnp.bfloat16)
                log = jnp.sum(jnp.where(column == first + h, logs, 0.0), axis=1, keepdims=True)
                state[span] = here * jnp.exp(log) + got[m, span].astype(jnp.float32)
            return carry

        lax.fori_loop(0, chips, one_chip, 0)
        for m in range(chips):
            outs[m][...] = given[m]

    return pl.pallas_call(
        kernel,
        out_shape=[shape((few * width, width), jnp.bfloat16)] * chips,
        in_specs=[SMEM] + [VMEM] * chips,
        out_specs=[VMEM] * chips,
        scratch_shapes=[
            pltpu.VMEM((chips, few * width + LOG_ROWS, width), jnp.bfloat16),
            pltpu.VMEM((chips, few * width, width), jnp.bfloat16),
            pltpu.VMEM((few * width, width), jnp.float32),
        ],
        compiler_params=params(24),
        cost_estimate=cost(2),
        name="scan_chips",
    )(place, *arrived)


def gather_entry(place, arrived):
    chips = len(arrived)
    width = arrived[0].shape[-1]
    few = arrived[0].shape[0] // width

    def kernel(place_ref, *rest):
        ins, out_ref = rest[:chips], rest[chips]
        chip = place_ref[0] // PAIR
        for m in range(chips):
            for h in range(few):
                out_ref[(chip ^ m) * few + h] = ins[m][span_of(h, width)]

    return pl.pallas_call(
        kernel,
        out_shape=shape((chips * few, width, width), jnp.bfloat16),
        in_specs=[SMEM] + [VMEM] * chips,
        out_specs=VMEM,
        compiler_params=params(16),
        cost_estimate=cost(1),
        name="gather_entry",
    )(place, *arrived)


def finish(place, queries, decay, across, gain, inner, entry_own, entry_other):
    rows, heads, width = queries.shape
    half = heads // PAIR
    slot = across.shape[0] - 1

    def kernel(
        place_ref, q_ref, decay_ref, gain_ref, inner_ref, own_ref, other_ref, across_ref, out_ref, mixed, near_decay, sem
    ):
        core = place_ref[0] % PAIR
        copy = pltpu.make_async_copy(across_ref.at[pl.ds(slot, 1)], near_decay, sem)
        copy.start()
        cumul, _ = decay_sums(decay_ref[...])
        copy.wait()
        near_sums, _ = decay_sums(near_decay[0, 0:heads, :])
        grown = jnp.exp(cumul + jnp.where(core == 0, 0.0, near_sums[rows - 1 : rows, :]))
        power = jnp.zeros((rows, width), jnp.float32)
        for at, step in turns(heads):
            q = jnp.swapaxes(q_ref[:, at : at + step, :], 0, 1)
            for h in range(step):
                i = at + h
                entry = jnp.where(core == i // half, own_ref[i % half], other_ref[i % half])
                mix = inner_ref[i] + nn(q[h], entry) * grown[:, i : i + 1]
                mixed[i] = mix
                power += mix * mix
        mean = jnp.sum(power, axis=1, keepdims=True) / (heads * width)
        norm = lax.rsqrt(mean + EPSILON)
        for at, step in turns(heads):
            normed = [
                (mixed[at + h] * norm * gain_ref[at + h : at + h + 1, :]).astype(jnp.bfloat16)
                for h in range(step)
            ]
            out_ref[:, at : at + step, :] = jnp.swapaxes(jnp.stack(normed), 0, 1)

    return pl.pallas_call(
        kernel,
        out_shape=shape((rows, heads, width), jnp.bfloat16),
        in_specs=[SMEM] + [VMEM] * 6 + [ANY],
        out_specs=VMEM,
        scratch_shapes=[
            pltpu.VMEM((heads, rows, width), jnp.float32),
            pltpu.VMEM((1, rows, width), jnp.bfloat16),
            pltpu.SemaphoreType.DMA,
        ],
        compiler_params=params(32),
        cost_estimate=cost(8),
        name="finish",
    )(place, queries, decay, gain, inner, entry_own, entry_other, across)


def per_device(
    lin_q, lin_k, lin_v, lin_decay, lin_gain, soft_q, soft_k, soft_v, block_bits, agent_ids
):
    count = lax.axis_size("seq")
    chips = count // PAIR
    rows, heads, width = soft_q.shape
    lin_heads = lin_q.shape[1]
    hosted = heads // chips
    place = lax.axis_index("seq").astype(jnp.int32).reshape(1)
    masks = range(1, chips)

    def exchange(value, m):
        return lax.ppermute(value, "seq", [(i, i ^ (PAIR * m)) for i in range(count)])

    def exchange_all(values):
        return [values[0]] + [exchange(values[m], m) for m in masks]

    def swap_cores(value):
        return lax.ppermute(value, "seq", [(i, i ^ 1) for i in range(count)])

    def after(value, *earlier):
        return lax.optimization_barrier((value, *earlier))[0]

    def together(values):
        return list(lax.optimization_barrier(tuple(values)))

    lin_decay = lin_decay.T
    near_k, near_v = swap_cores(lin_k), swap_cores(lin_v)
    packed = pack(place, (soft_q, soft_k, soft_v), lin_decay, chips)
    across = swap_cores(packed[0])
    totals = totals_of(place, lin_k, lin_v, lin_decay, near_k, near_v, across, chips)
    own = exchange_all([*packed[:-1], after(packed[-1], totals[0])])
    totals = exchange_all(totals)
    inner = within(place, lin_q, lin_k, lin_v, lin_decay, near_k, near_v, after(across, totals[0]))
    arrived = together([*own, *totals, inner])
    own, totals, inner = arrived[:chips], arrived[chips:-1], arrived[-1]
    other = [across] + [swap_cores(block) for block in own[1:]]
    starts = scan_chips(place, totals, lin_heads)

    entries = exchange_all(starts)
    mixed = attend(place, block_bits, agent_ids, own, other, hosted)
    back = exchange_all(mixed)
    entry = gather_entry(place, [after(block, mixed[0]) for block in entries])
    gain = lin_gain.reshape(lin_heads, width)
    lin_out = finish(place, lin_q, lin_decay, across, gain, inner, entry, swap_cores(entry))
    back[0] = after(back[0], lin_out)
    soft_out = unpack(place, back, heads, rows)
    return (lin_out, soft_out)


def solution(mesh):
    rows = P(("dp", "seq"), None, None)
    return jax.shard_map(
        per_device,
        mesh=mesh,
        in_specs=(rows, rows, rows, P(("dp", "seq"), None), P(), rows, rows, rows, P("dp", None), P("dp")),
        out_specs=(rows, rows),
        check_vma=False,
    )
```

```python
import jax
import jax.numpy as jnp
from jax import lax
from jax.experimental import pallas as pl
from jax.experimental.pallas import tpu as pltpu
from jax.sharding import PartitionSpec as P

EPSILON = 1e-06
PAIR = 2
WEIGHT = 1 << 31
TURN = 16
LOG_ROWS = 16
LOG2E = 1.4426950408889634
VMEM = pl.BlockSpec(memory_space=pltpu.VMEM)
SMEM = pl.BlockSpec(memory_space=pltpu.SMEM)
ANY = pl.BlockSpec(memory_space=pl.ANY)
HBM = pl.BlockSpec(memory_space=pltpu.HBM)


def params(mib):
    return pltpu.CompilerParams(vmem_limit_bytes=mib << 20)


def cost(weight=1):
    return pl.CostEstimate(flops=WEIGHT * weight, bytes_accessed=1, transcendentals=0)


def shape(dims, dtype):
    return jax.ShapeDtypeStruct(dims, dtype)


def turns(heads):
    step = min(TURN, heads)
    return [(at, step) for at in range(0, heads, step)]


def span_of(index, rows):
    return pl.ds(index * rows, rows)


def nt(a, b):
    return lax.dot_general(a, b, (((1,), (1,)), ((), ())), preferred_element_type=jnp.float32)


def tn(a, b):
    return lax.dot_general(a, b, (((0,), (0,)), ((), ())), preferred_element_type=jnp.float32)


def nn(a, b):
    return lax.dot_general(a, b, (((1,), (0,)), ((), ())), preferred_element_type=jnp.float32)


def triangle(size):
    rows = lax.broadcasted_iota(jnp.int32, (size, size), 0)
    cols = lax.broadcasted_iota(jnp.int32, (size, size), 1)
    return cols <= rows


def pack(place, arrays, decay, chips):
    rows, heads, width = arrays[0].shape
    hosted, lin_heads = heads // chips, decay.shape[0]
    pieces = 2
    cut = rows // pieces

    def kernel(place_ref, decay_ref, q_ref, k_ref, v_ref, *rest):
        outs, (landed, turned, in_sems, out_sems, decay_sem) = rest[:-5], rest[-5:]
        chip = place_ref[0] // PAIR
        order = [(1, k_ref), (0, q_ref), (2, v_ref)]
        arriving = {}
        for which, ref in order:
            for piece in range(pieces):
                span = pl.ds(piece * cut, cut)
                arriving[which, piece] = pltpu.make_async_copy(
                    ref.at[span], landed.at[which, span], in_sems.at[which, piece]
                )
                arriving[which, piece].start()
        leaving = [
            pltpu.make_async_copy(decay_ref, outs[0].at[3 * hosted, pl.ds(0, lin_heads)], decay_sem)
        ]
        leaving[-1].start()

        def send(which, piece, span):
            for m in range(chips):
                leaving.append(
                    pltpu.make_async_copy(
                        turned.at[which, pl.ds((chip ^ m) * hosted, hosted), span],
                        outs[m].at[pl.ds(which * hosted, hosted), span],
                        out_sems.at[which, piece, m],
                    )
                )
                leaving[-1].start()

        for which, _ in order:
            for piece in range(pieces):
                arriving[which, piece].wait()
                if which == 1:
                    continue
                at_rows = slice(piece * cut, (piece + 1) * cut)
                for at, step in turns(heads):
                    block = jnp.swapaxes(landed[which, at_rows, at : at + step, :], 0, 1)
                    turned[which, at : at + step, at_rows, :] = block
                send(which, piece, pl.ds(piece * cut, cut))
            if which == 1:
                for at, step in turns(heads):
                    block = jnp.swapaxes(landed[which, :, at : at + step, :], 0, 1)
                    for h in range(step):
                        turned[which, at + h] = block[h].T
                send(which, 0, pl.ds(0, rows))
        for copy in leaving:
            copy.wait()

    return pl.pallas_call(
        kernel,
        out_shape=[shape((3 * hosted + (m == 0), rows, width), jnp.bfloat16) for m in range(chips)],
        in_specs=[SMEM, ANY, ANY, ANY, ANY],
        out_specs=[ANY] * chips,
        scratch_shapes=[
            pltpu.VMEM((3, rows, heads, width), jnp.bfloat16),
            pltpu.VMEM((3, heads, rows, width), jnp.bfloat16),
            pltpu.SemaphoreType.DMA((3, pieces)),
            pltpu.SemaphoreType.DMA((3, pieces, chips)),
            pltpu.SemaphoreType.DMA,
        ],
        compiler_params=params(56),
        cost_estimate=cost(4),
        name="pack",
    )(place, decay, *arrays)


def attend(place, bits, agents, own, other, each):
    chips = len(own)
    _, rows, width = own[0].shape
    slots = PAIR * chips
    scale = width**-0.5 * LOG2E
    most = sum(PAIR * chip + PAIR - 1 for chip in range(chips))

    def kernel(place_ref, bits_ref, agents_ref, *rest):
        ins, outs = rest[:slots], rest[slots : slots + chips]
        queries, scores, top, total, mixed, probs, query_of = rest[slots + chips :]
        me = place_ref[0]
        chip, core = me // PAIR, me % PAIR

        found, ends = jnp.int32(0), []
        for j in range(slots):
            key_block = PAIR * (chip ^ (j % chips)) + (core if j < chips else PAIR - 1 - core)

            for i in range(chips):
                query_block = PAIR * (chip ^ i) + core
                seen = (key_block < query_block) & (
                    (bits_ref[query_block, key_block] == 1) | (agents_ref[query_block] == agents_ref[key_block])
                )
                query_of[found] = i
                found = found + seen.astype(jnp.int32)
            ends.append(found)

        lower = triangle(rows)
        for i in range(chips):
            for h in range(each):
                queries[i, h] = ins[i][h]
                top[i, h] = jnp.where(lower, nn(ins[i][h], ins[i][each + h]), -1e30)
        for i in range(chips):
            for h in range(each):
                total[i, h] = top[i, h]

        for j in range(slots):

            def score(at, carry, j=j):
                i = query_of[at]
                for h in range(each):
                    s = nn(queries[i, h], ins[j][each + h])
                    scores[at, h] = s
                    top[i, h] = jnp.maximum(top[i, h], s)
                return carry

            lax.fori_loop(ends[j - 1] if j else 0, ends[j], score, 0)

        for i in range(chips):
            for h in range(each):
                top[i, h] = jnp.broadcast_to(jnp.max(top[i, h], axis=1, keepdims=True), (rows, rows))
        for i in range(chips):
            for h in range(each):
                p = jnp.exp2((total[i, h] - top[i, h]) * scale)
                total[i, h] = p
                probs[i, h] = p.astype(jnp.bfloat16)
        for i in range(chips):
            for h in range(each):
                mixed[i, h] = nn(probs[i, h], ins[i][2 * each + h])

        for j in range(slots):

            def weigh(at, carry, j=j):
                i = query_of[at]
                for h in range(each):
                    p = jnp.exp2((scores[at, h] - top[i, h]) * scale)
                    total[i, h] += p
                    probs[0, h] = p.astype(jnp.bfloat16)
                for h in range(each):
                    mixed[i, h] += nn(probs[0, h], ins[j][2 * each + h])
                return carry

            lax.fori_loop(ends[j - 1] if j else 0, ends[j], weigh, 0)

        for i in range(chips):
            for h in range(each):
                sums = jnp.sum(total[i, h], axis=1, keepdims=True)
                outs[i][span_of(h, rows)] = (mixed[i, h] / sums).astype(jnp.bfloat16)

    block = (chips, each, rows, rows)
    in_bytes = 2 * each * rows * (3 * slots * width + 3 * chips * rows)
    score_bytes = 4 * each * rows * ((most + 2 * chips) * rows + chips * width)
    return pl.pallas_call(
        kernel,
        out_shape=[shape((each * rows, width), jnp.bfloat16)] * chips,
        in_specs=[SMEM, SMEM, SMEM] + [VMEM] * slots,
        out_specs=[VMEM] * chips,
        scratch_shapes=[
            pltpu.VMEM((chips, each, rows, width), jnp.bfloat16),
            pltpu.VMEM((most, each, rows, rows), jnp.float32),
            pltpu.VMEM(block, jnp.float32),
            pltpu.VMEM(block, jnp.float32),
            pltpu.VMEM((chips, each, rows, width), jnp.float32),
            pltpu.VMEM(block, jnp.bfloat16),
            pltpu.SMEM((most + 1,), jnp.int32),
        ],
        compiler_params=params(6 + (in_bytes + score_bytes >> 20)),
        cost_estimate=cost(14),
        name="attend",
    )(place, bits, agents, *own, *other)


def unpack(place, pieces, heads, rows):
    chips, width = len(pieces), pieces[0].shape[-1]
    hosted = heads // chips

    def kernel(place_ref, *rest):
        ins, out_ref, turned = rest[:-2], rest[-2], rest[-1]
        chip = place_ref[0] // PAIR
        for m in range(chips):
            for h in range(hosted):
                turned[(chip ^ m) * hosted + h] = ins[m][span_of(h, rows)]
        for at, step in turns(heads):
            out_ref[:, at : at + step, :] = jnp.swapaxes(turned[at : at + step], 0, 1)

    return pl.pallas_call(
        kernel,
        out_shape=shape((rows, heads, width), jnp.bfloat16),
        in_specs=[SMEM] + [VMEM] * chips,
        out_specs=VMEM,
        scratch_shapes=[pltpu.VMEM((heads, rows, width), jnp.bfloat16)],
        compiler_params=params(16),
        cost_estimate=cost(4),
        name="unpack",
    )(place, *pieces)


def decay_sums(decay):
    lower = triangle(decay.shape[1]).astype(jnp.bfloat16)
    return nt(lower, decay), nt(decay, lower)


def block_state(key, value, left):
    return tn((key.astype(jnp.float32) * left).astype(jnp.bfloat16), value)


def totals_of(place, keys, values, decay, near_keys, near_values, across, chips):
    rows, heads, width = keys.shape
    half = heads // PAIR
    few = half // chips
    slot = across.shape[0] - 1

    def kernel(place_ref, k_ref, v_ref, decay_ref, near_k_ref, near_v_ref, across_ref, *rest):
        outs, (turned, near_decay, totals, sem) = rest[:chips], rest[chips:]
        core, chip = place_ref[0] % PAIR, place_ref[0] // PAIR
        copy = pltpu.make_async_copy(across_ref.at[pl.ds(slot, 1)], near_decay, sem)
        copy.start()
        for which, ref in enumerate((k_ref, v_ref, near_k_ref, near_v_ref)):
            for at, step in turns(heads):
                turned[which, at : at + step] = jnp.swapaxes(ref[:, at : at + step, :], 0, 1)
        copy.wait()
        own_sums, _ = decay_sums(decay_ref[...])
        near_sums, _ = decay_sums(near_decay[0, 0:heads, :])
        own_last, near_last = own_sums[rows - 1 : rows, :], near_sums[rows - 1 : rows, :]
        own_left = jnp.exp(own_last - own_sums)
        near_left = jnp.exp(near_last - near_sums)
        own_then = jnp.where(core == 0, jnp.exp(near_last), 1.0)
        near_then = jnp.where(core == 0, 1.0, jnp.exp(own_last))

        def half_of(sums):
            return jnp.where(core == 0, sums[:, 0:half], sums[:, half:heads])

        own_left, near_left, own_then, near_then = map(half_of, (own_left, near_left, own_then, near_then))
        for h in range(half):
            at = core * half + h
            own = block_state(turned[0, at], turned[1, at], own_left[:, h : h + 1])
            near = block_state(turned[2, at], turned[3, at], near_left[:, h : h + 1])
            total = own * own_then[:, h : h + 1] + near * near_then[:, h : h + 1]
            totals[h] = total.astype(jnp.bfloat16)
        logs = jnp.concatenate([own_last + near_last, jnp.zeros((1, width - heads), jnp.float32)], axis=1)
        first = logs.astype(jnp.bfloat16).astype(jnp.float32)
        second = (logs - first).astype(jnp.bfloat16).astype(jnp.float32)
        third = logs - first - second
        row = lax.broadcasted_iota(jnp.int32, (LOG_ROWS, width), 0)
        split = jnp.where(row == 0, first, jnp.where(row == 1, second, jnp.where(row == 2, third, 0.0)))
        for m in range(chips):
            for h in range(few):
                outs[m][span_of(h, width)] = totals[(chip ^ m) * few + h]
            outs[m][few * width :] = split.astype(jnp.bfloat16)

    return pl.pallas_call(
        kernel,
        out_shape=[shape((few * width + LOG_ROWS, width), jnp.bfloat16)] * chips,
        in_specs=[SMEM] + [VMEM] * 5 + [ANY],
        out_specs=[VMEM] * chips,
        scratch_shapes=[
            pltpu.VMEM((4, heads, rows, width), jnp.bfloat16),
            pltpu.VMEM((1, rows, width), jnp.bfloat16),
            pltpu.VMEM((half, width, width), jnp.bfloat16),
            pltpu.SemaphoreType.DMA,
        ],
        compiler_params=params(24),
        cost_estimate=cost(6),
        name="totals_of",
    )(place, keys, values, decay, near_keys, near_values, across)


def within(place, queries, keys, values, decay, near_keys, near_values, across):
    rows, heads, width = queries.shape
    slot = across.shape[0] - 1

    def kernel(place_ref, q_ref, k_ref, v_ref, decay_ref, near_k_ref, near_v_ref, across_ref, out_ref, near_decay, sem):
        core = place_ref[0] % PAIR
        copy = pltpu.make_async_copy(across_ref.at[pl.ds(slot, 1)], near_decay, sem)
        copy.start()
        cumul, cumul_row = decay_sums(decay_ref[...])
        grown = jnp.exp(cumul)
        lower = triangle(rows)
        for at, step in turns(heads):
            q = jnp.swapaxes(q_ref[:, at : at + step, :], 0, 1)
            k = jnp.swapaxes(k_ref[:, at : at + step, :], 0, 1)
            v = jnp.swapaxes(v_ref[:, at : at + step, :], 0, 1)
            for h in range(step):
                i = at + h
                apart = cumul[:, i : i + 1] - cumul_row[i : i + 1, :]
                damping = jnp.where(lower, jnp.exp(jnp.where(lower, apart, 0.0)), 0.0)
                weights = (nt(q[h], k[h]) * damping).astype(jnp.bfloat16)
                out_ref[i] = nn(weights, v[h])
        copy.wait()

        @pl.when(core > 0)
        def _():
            near_sums, _ = decay_sums(near_decay[0, 0:heads, :])
            left = jnp.exp(near_sums[rows - 1 : rows, :] - near_sums)
            for at, step in turns(heads):
                q = jnp.swapaxes(q_ref[:, at : at + step, :], 0, 1)
                k = jnp.swapaxes(near_k_ref[:, at : at + step, :], 0, 1)
                v = jnp.swapaxes(near_v_ref[:, at : at + step, :], 0, 1)
                for h in range(step):
                    i = at + h
                    state = block_state(k[h], v[h], left[:, i : i + 1])
                    out_ref[i] += precisely(q[h], state) * grown[:, i : i + 1]

    return pl.pallas_call(
        kernel,
        out_shape=shape((heads, rows, width), jnp.float32),
        in_specs=[SMEM] + [VMEM] * 6 + [ANY],
        out_specs=VMEM,
        scratch_shapes=[pltpu.VMEM((1, rows, width), jnp.bfloat16), pltpu.SemaphoreType.DMA],
        compiler_params=params(24),
        cost_estimate=cost(14),
        name="within",
    )(place, queries, keys, values, decay, near_keys, near_values, across)


def precisely(q, state):
    coarse = state.astype(jnp.bfloat16)
    fine = (state - coarse.astype(jnp.float32)).astype(jnp.bfloat16)
    return nn(q, coarse) + nn(q, fine)


def scan_chips(place, arrived, heads):
    chips = len(arrived)
    width = arrived[0].shape[-1]
    half = heads // PAIR
    few = half // chips

    def kernel(place_ref, *rest):
        ins, outs = rest[:chips], rest[chips : 2 * chips]
        got, given, state = rest[2 * chips :]
        core, chip = place_ref[0] % PAIR, place_ref[0] // PAIR
        for m in range(chips):
            got[m] = ins[m][...]
        state[...] = jnp.zeros_like(state)
        column = lax.broadcasted_iota(jnp.int32, (1, width), 1)
        first = core * half + chip * few

        def one_chip(c, carry):
            m = c ^ chip
            logs = jnp.sum(got[m, few * width :].astype(jnp.float32), axis=0, keepdims=True)
            for h in range(few):
                span = span_of(h, width)
                here = state[span]
                given[m, span] = here.astype(jnp.bfloat16)
                log = jnp.sum(jnp.where(column == first + h, logs, 0.0), axis=1, keepdims=True)
                state[span] = here * jnp.exp(log) + got[m, span].astype(jnp.float32)
            return carry

        lax.fori_loop(0, chips, one_chip, 0)
        for m in range(chips):
            outs[m][...] = given[m]

    return pl.pallas_call(
        kernel,
        out_shape=[shape((few * width, width), jnp.bfloat16)] * chips,
        in_specs=[SMEM] + [VMEM] * chips,
        out_specs=[VMEM] * chips,
        scratch_shapes=[
            pltpu.VMEM((chips, few * width + LOG_ROWS, width), jnp.bfloat16),
            pltpu.VMEM((chips, few * width, width), jnp.bfloat16),
            pltpu.VMEM((few * width, width), jnp.float32),
        ],
        compiler_params=params(24),
        cost_estimate=cost(2),
        name="scan_chips",
    )(place, *arrived)


def gather_entry(place, arrived):
    chips = len(arrived)
    width = arrived[0].shape[-1]
    few = arrived[0].shape[0] // width

    def kernel(place_ref, *rest):
        ins, out_ref = rest[:chips], rest[chips]
        chip = place_ref[0] // PAIR
        for m in range(chips):
            for h in range(few):
                out_ref[(chip ^ m) * few + h] = ins[m][span_of(h, width)]

    return pl.pallas_call(
        kernel,
        out_shape=shape((chips * few, width, width), jnp.bfloat16),
        in_specs=[SMEM] + [VMEM] * chips,
        out_specs=VMEM,
        compiler_params=params(16),
        cost_estimate=cost(1),
        name="gather_entry",
    )(place, *arrived)


def finish(place, queries, decay, across, gain, inner, entry_own, entry_other):
    rows, heads, width = queries.shape
    half = heads // PAIR
    slot = across.shape[0] - 1

    def kernel(
        place_ref, q_ref, decay_ref, gain_ref, inner_ref, own_ref, other_ref, across_ref, out_ref, mixed, near_decay, sem
    ):
        core = place_ref[0] % PAIR
        copy = pltpu.make_async_copy(across_ref.at[pl.ds(slot, 1)], near_decay, sem)
        copy.start()
        cumul, _ = decay_sums(decay_ref[...])
        copy.wait()
        near_sums, _ = decay_sums(near_decay[0, 0:heads, :])
        grown = jnp.exp(cumul + jnp.where(core == 0, 0.0, near_sums[rows - 1 : rows, :]))
        power = jnp.zeros((rows, width), jnp.float32)
        for at, step in turns(heads):
            q = jnp.swapaxes(q_ref[:, at : at + step, :], 0, 1)
            for h in range(step):
                i = at + h
                entry = jnp.where(core == i // half, own_ref[i % half], other_ref[i % half])
                mix = inner_ref[i] + nn(q[h], entry) * grown[:, i : i + 1]
                mixed[i] = mix
                power += mix * mix
        mean = jnp.sum(power, axis=1, keepdims=True) / (heads * width)
        norm = lax.rsqrt(mean + EPSILON)
        for at, step in turns(heads):
            normed = [
                (mixed[at + h] * norm * gain_ref[at + h : at + h + 1, :]).astype(jnp.bfloat16)
                for h in range(step)
            ]
            out_ref[:, at : at + step, :] = jnp.swapaxes(jnp.stack(normed), 0, 1)

    return pl.pallas_call(
        kernel,
        out_shape=shape((rows, heads, width), jnp.bfloat16),
        in_specs=[SMEM] + [VMEM] * 6 + [ANY],
        out_specs=VMEM,
        scratch_shapes=[
            pltpu.VMEM((heads, rows, width), jnp.float32),
            pltpu.VMEM((1, rows, width), jnp.bfloat16),
            pltpu.SemaphoreType.DMA,
        ],
        compiler_params=params(32),
        cost_estimate=cost(8),
        name="finish",
    )(place, queries, decay, gain, inner, entry_own, entry_other, across)


def per_device(
    lin_q, lin_k, lin_v, lin_decay, lin_gain, soft_q, soft_k, soft_v, block_bits, agent_ids
):
    count = lax.axis_size("seq")
    chips = count // PAIR
    rows, heads, width = soft_q.shape
    lin_heads = lin_q.shape[1]
    hosted = heads // chips
    place = lax.axis_index("seq").astype(jnp.int32).reshape(1)
    masks = range(1, chips)

    def exchange(value, m):
        return lax.ppermute(value, "seq", [(i, i ^ (PAIR * m)) for i in range(count)])

    def exchange_all(values):
        return [values[0]] + [exchange(values[m], m) for m in masks]

    def swap_cores(value):
        return lax.ppermute(value, "seq", [(i, i ^ 1) for i in range(count)])

    def after(value, *earlier):
        return lax.optimization_barrier((value, *earlier))[0]

    def together(values):
        return list(lax.optimization_barrier(tuple(values)))

    lin_decay = lin_decay.T
    near_k, near_v = swap_cores(lin_k), swap_cores(lin_v)
    packed = pack(place, (soft_q, soft_k, soft_v), lin_decay, chips)
    across = swap_cores(packed[0])
    totals = totals_of(place, lin_k, lin_v, lin_decay, near_k, near_v, across, chips)
    own = exchange_all([*packed[:-1], after(packed[-1], totals[0])])
    totals = exchange_all(totals)
    inner = within(place, lin_q, lin_k, lin_v, lin_decay, near_k, near_v, after(across, totals[0]))
    arrived = together([*own, *totals, inner])
    own, totals, inner = arrived[:chips], arrived[chips:-1], arrived[-1]
    other = [across] + [swap_cores(block) for block in own[1:]]
    starts = scan_chips(place, totals, lin_heads)

    entries = exchange_all(starts)
    mixed = attend(place, block_bits, agent_ids, own, other, hosted)
    back = exchange_all(mixed)
    entry = gather_entry(place, [after(block, mixed[0]) for block in entries])
    gain = lin_gain.reshape(lin_heads, width)
    lin_out = finish(place, lin_q, lin_decay, across, gain, inner, entry, swap_cores(entry))
    back[0] = after(back[0], lin_out)
    soft_out = unpack(place, back, heads, rows)
    return (lin_out, soft_out)


def solution(mesh):
    rows = P(("dp", "seq"), None, None)
    return jax.shard_map(
        per_device,
        mesh=mesh,
        in_specs=(rows, rows, rows, P(("dp", "seq"), None), P(), rows, rows, rows, P("dp", None), P("dp")),
        out_specs=(rows, rows),
        check_vma=False,
    )
```
